32 devices in a mesh: dp: 2 (over y), ctx: 8 (over z, x), tp: 2 (over core).
Axes of the slice: x: 2, y: 2, z: 4, core: 2. Of those that a mesh axis runs over, the one named last changes fastest.
Arguments:
- inputs: bfloat16 [2, 1024, 768], P('dp', 'ctx'), may hold values from -6 to 6
- segments: int32 [2, 1024], P('dp', 'ctx'), may hold values from 0 to 2, as said below
- gain_one: float32 [768], replicated, may hold values from 0.5 to 1.5
- bias_one: float32 [768], replicated, may hold values from -1.5 to 1.5
- gain_two: float32 [768], replicated, may hold values from 0.5 to 1.5
- bias_two: float32 [768], replicated, may hold values from -1.5 to 1.5
- w_qkv: bfloat16 [768, 3, 768], P(('dp', 'ctx'), None, 'tp'), may hold values from -0.21875 to 0.21875
- b_qkv: float32 [3, 768], P(None, 'tp'), may hold values from -0.5 to 0.5
- w_out: bfloat16 [768, 768], P(('dp', 'ctx'), 'tp'), may hold values from -1.75 to 1.75
- out_bias: float32 [768], replicated, may hold values from -1.5 to 1.5
- w_up: bfloat16 [768, 3072], P(('dp', 'ctx'), 'tp'), may hold values from -0.21875 to 0.21875
- b_up: float32 [3072], P('tp'), may hold values from -1.5 to 1.5
- w_down: bfloat16 [768, 3072], P(('dp', 'ctx'), 'tp'), may hold values from -0.109375 to 0.109375
- cotangent: bfloat16 [2, 1024, 768], P('dp', 'ctx'), may hold values from -6 to 6
Outputs:
- output: float32 [2, 1024, 768], P('dp', 'ctx', 'tp')
- grad_inputs: float32 [2, 1024, 768], P('dp', 'ctx', 'tp')
- grad_gain_one: float32 [768], replicated
- grad_bias_one: float32 [768], replicated
- grad_gain_two: float32 [768], replicated
- grad_bias_two: float32 [768], replicated
- grad_w_qkv: float32 [768, 3, 768], P(('dp', 'ctx'), None, 'tp')
- grad_b_qkv: float32 [3, 768], P(None, 'tp')
- grad_w_out: float32 [768, 768], P(('dp', 'ctx'), 'tp')
- grad_out_bias: float32 [768], replicated
- grad_w_up: float32 [768, 3072], P(('dp', 'ctx'), 'tp')
- grad_b_up: float32 [3072], P('tp')
- grad_w_down: float32 [768, 3072], P(('dp', 'ctx'), 'tp')
The draws below stay inside these ranges and needn't reach their ends.
Inputs may be any that keep to these rules, and one draw needn't show every extreme that they name: `segments`: in every row the segment numbers are 0, 1 and 2, all three present, never falling along the row; the first and the last segment each hold 1 to 64 tokens.
All inputs are finite; a program needn't handle non-finite values.
Results may differ from the reference program's by a relative error of at most 0.012.
Values may be sent and summed in bfloat16 or wider, within the bound.
A program may use at most 128 MiB of HBM per device.

```python
import math
import jax
import jax.numpy as jnp
from jax import lax

D = 768
HD = 64
ROT = 16
FF = 3072
TOK_DEV = 128
ROWS = 2
LEN = 1024


def draw_segments(key, part):
    key = jax.random.fold_in(key, 11)
    first_key, second_key = jax.random.split(key)
    border = max(1, TOK_DEV // 2)
    head_len = jax.random.randint(first_key, (ROWS, 1), 1, border + 1)
    tail_len = jax.random.randint(second_key, (ROWS, 1), 1, border + 1)
    position = jnp.arange(LEN)[None, :]
    return (position >= head_len).astype(jnp.int32) + (position >= LEN - tail_len).astype(jnp.int32)


def levels(own_key, shape, cuts, least, top_value):
    def one(dim, parts):
        steps = jax.random.uniform(jax.random.fold_in(jax.random.fold_in(own_key, 6), dim), (parts,), jnp.float32, least / len(cuts), top_value / len(cuts))
        return jnp.repeat(jnp.exp(steps), shape[dim] // parts).reshape((-1,) + (1,) * (len(shape) - dim - 1))

    gain = one(*cuts[0])
    for cut in cuts[1:]:
        gain = gain * one(*cut)
    return gain


def centred(own_key, extent, spread, reach, cuts=(), kind=jnp.bfloat16):
    entries = jax.random.normal(own_key, extent, jnp.float32) * spread
    if len(cuts) > 0:
        entries = levels(own_key, extent, cuts, -0.22, 0.18) * entries
    return jnp.clip(entries, min=-reach, max=reach).astype(kind)


def setup_inputs(seed: int = 0) -> dict:
    key_of = jax.random.split(jax.random.key(seed), 15)
    inputs = centred(key_of[0], (ROWS, LEN, D), 1.0, 6.0, ((0, 2), (1, 8)))
    segments = draw_segments(jax.random.fold_in(key_of[14], 71), 0)
    gain_one = jnp.clip(1.0 + 0.1 * jax.random.normal(key_of[2], (D,), jnp.float32), 0.5, 1.5)
    bias_one = centred(key_of[3], (D,), 0.3, 1.5, (), jnp.float32)
    gain_two = jnp.clip(1.0 + 0.1 * jax.random.normal(key_of[4], (D,), jnp.float32), 0.5, 1.5)
    bias_two = centred(key_of[5], (D,), 0.3, 1.5, (), jnp.float32)
    w_qkv = centred(key_of[6], (D, 3, D), D ** -0.5, 0.21875, ((0, 16), (2, 2)))
    b_qkv = centred(key_of[7], (3, D), 0.1, 0.5, ((1, 2),), jnp.float32)
    w_out = centred(key_of[8], (D, D), (D // 64) ** -0.5, 1.75, ((0, 16), (1, 2)))
    out_bias = centred(key_of[9], (D,), 0.3, 1.5, (), jnp.float32)
    w_up = centred(key_of[10], (D, FF), D ** -0.5, 0.21875, ((0, 16), (1, 2)))
    b_up = centred(key_of[11], (FF,), 0.3, 1.5, ((0, 2),), jnp.float32)
    w_down = centred(key_of[12], (D, FF), FF ** -0.5, 0.109375, ((0, 16), (1, 2)))
    cotangent = centred(key_of[13], (ROWS, LEN, D), 1.0, 6.0, ((0, 2), (1, 8)))
    return {"inputs": inputs, "segments": segments, "gain_one": gain_one, "bias_one": bias_one, "gain_two": gain_two, "bias_two": bias_two, "w_qkv": w_qkv, "b_qkv": b_qkv, "w_out": w_out, "out_bias": out_bias, "w_up": w_up, "b_up": b_up, "w_down": w_down, "cotangent": cotangent}


@jax.custom_vjp
def low(v):
    return lax.optimization_barrier(v.astype(jnp.bfloat16)).astype(jnp.float32)

@jax.custom_vjp
def low_back(v):
    return v

def low_keep(v):
    return (low(v), None)

def low_pass(kept, grad):
    return (grad,)

def back_keep(v):
    return (v, None)

def back_low(kept, grad):
    return (low(grad),)
low.defvjp(low_keep, low_pass)
low_back.defvjp(back_keep, back_low)
NORM_EPSILON = 1e-05
NEG_LARGE = -1e+30

def layer_norm(values, norm_gain, norm_bias):
    average = lax.optimization_barrier(jnp.mean(values, axis=-1, keepdims=True))
    centered = values - average
    variance = lax.optimization_barrier(jnp.mean(centered * centered, axis=-1, keepdims=True))
    return centered * lax.rsqrt(variance + NORM_EPSILON) * norm_gain + norm_bias

def angle_tables(first_row, length):
    positions = (first_row + jnp.arange(length)).astype(jnp.float32)
    frequency = 10000.0 ** (-(jnp.arange(ROT // 2).astype(jnp.float32) * 2.0 / ROT))
    angles = positions[:, None] * frequency[None, :]
    return (jnp.cos(angles)[:, None, :], jnp.sin(angles)[:, None, :])

def rotate(values, cosine_table, sine_table):
    half_rot = cosine_table.shape[-1]
    lower = values[..., :half_rot]
    upper = values[..., half_rot:2 * half_rot]
    return jnp.concatenate([lower * cosine_table - upper * sine_table, upper * cosine_table + lower * sine_table, values[..., 2 * half_rot:]], axis=-1)

def head_attention(queries, key_rows, value_rows, seg_row):
    length = queries.shape[0]
    block_size = math.gcd(length, 1024)
    position = jnp.arange(length)
    softmax_scale = 1.0 / math.sqrt(HD)
    results = []
    for first_row in range(0, length, block_size):
        last_row = first_row + block_size
        scores = jnp.dot(queries[first_row:last_row], key_rows[:last_row].T, precision=lax.Precision.HIGHEST) * softmax_scale
        scores = low_back(scores)
        allowed = (position[None, :last_row] <= position[first_row:last_row, None]) & (seg_row[None, :last_row] == seg_row[first_row:last_row, None])
        scores = jnp.where(allowed, scores, NEG_LARGE)
        top_score = lax.optimization_barrier(jnp.max(scores, axis=-1, keepdims=True))
        exponent = jnp.exp(scores - top_score)
        probability = low(exponent / lax.optimization_barrier(jnp.sum(exponent, axis=-1, keepdims=True)))
        results.append(jnp.dot(probability, value_rows[:last_row], precision=lax.Precision.HIGHEST))
    return jnp.concatenate(results, axis=0)

def row_attention(row_items):
    queries, key_rows, value_rows, seg_row = row_items
    per_head = jax.checkpoint(lambda triple_item: head_attention(triple_item[0], triple_item[1], triple_item[2], seg_row))
    heads_out = lax.map(per_head, (jnp.swapaxes(queries, 0, 1), jnp.swapaxes(key_rows, 0, 1), jnp.swapaxes(value_rows, 0, 1)))
    return jnp.swapaxes(heads_out, 0, 1)

def forward(inputs, gain_one, bias_one, gain_two, bias_two, w_qkv, b_qkv, w_out, out_bias, w_up, b_up, w_down, segments):
    precise = lax.Precision.HIGHEST
    row_count, length, model_width = inputs.shape
    norm_one = low(layer_norm(inputs, gain_one, bias_one))
    norm_two = low(layer_norm(inputs, gain_two, bias_two))
    projected = low_back(jnp.einsum('rld,dcm->rlcm', norm_one, w_qkv, precision=precise) + b_qkv)
    shaped = projected.reshape(row_count, length, 3, model_width // HD, HD)
    cosine_table, sine_table = angle_tables(0, length)
    queries = low(rotate(shaped[:, :, 0], cosine_table, sine_table))
    key_rows = low(rotate(shaped[:, :, 1], cosine_table, sine_table))
    value_rows = low(shaped[:, :, 2])
    attended = lax.map(row_attention, (queries, key_rows, value_rows, segments))
    attended = low_back(low(attended.reshape(row_count, length, model_width)))
    attn_branch = jnp.einsum('rlf,df->rld', attended, w_out, precision=precise)
    pre_gelu = low_back(jnp.einsum('rld,df->rlf', norm_two, w_up, precision=precise) + b_up)
    activated = low(jax.nn.gelu(pre_gelu, approximate=False))
    mlp_branch = jnp.einsum('rlf,df->rld', activated, w_down, precision=precise)
    return inputs + attn_branch + mlp_branch + out_bias

def reference(inputs, segments, gain_one, bias_one, gain_two, bias_two, w_qkv, b_qkv, w_out, out_bias, w_up, b_up, w_down, cotangent):
    params = (inputs.astype(jnp.float32), gain_one, bias_one, gain_two, bias_two, w_qkv.astype(jnp.float32), b_qkv, w_out.astype(jnp.float32), out_bias, w_up.astype(jnp.float32), b_up, w_down.astype(jnp.float32))
    output, pullback = jax.vjp(lambda *arguments: forward(*arguments, segments), *params)
    gradients = pullback(cotangent.astype(jnp.float32))
    return (output, gradients[0], gradients[1], gradients[2], gradients[3], gradients[4], gradients[5], gradients[6], gradients[7], gradients[8], gradients[9], gradients[10], gradients[11])
```

```python
import math

import jax
import jax.numpy as jnp
from jax import lax
from jax.sharding import PartitionSpec as P

HD = 64
ROT = 16

NORM_EPSILON = 1e-05
NEG_LARGE = -1e30
LAST = (((1,), (1,)), ((), ()))
ROWS = (((0,), (0,)), ((), ()))


def dot_f32(a, b, dims=(((1,), (0,)), ((), ()))):
    return lax.dot_general(a, b, dims, preferred_element_type=jnp.float32)


def angle_tables(first_row, length):
    positions = (first_row + jnp.arange(length)).astype(jnp.float32)
    frequency = 10000.0 ** (-(jnp.arange(ROT // 2).astype(jnp.float32) * 2.0 / ROT))
    angles = positions[:, None] * frequency[None, :]
    return (jnp.cos(angles), jnp.sin(angles))


def rotate(values, cosine_table, sine_table):
    half_rot = ROT // 2
    lower = values[..., :half_rot]
    upper = values[..., half_rot : 2 * half_rot]
    return jnp.concatenate(
        [
            lower * cosine_table - upper * sine_table,
            upper * cosine_table + lower * sine_table,
            values[..., 2 * half_rot :],
        ],
        axis=-1,
    )


def gather_tokens(packed):
    return lax.all_gather(packed, "ctx", axis=0, tiled=True)


def weights_to_columns(blocks):
    received = lax.all_to_all(blocks, "ctx", 0, 0, tiled=True)
    return lax.all_gather(received, "dp", axis=0, tiled=False)


def grads_to_owners(blocks):
    dp, ctx = blocks.shape[:2]
    mine = lax.psum_scatter(blocks, "dp", scatter_dimension=0, tiled=False)
    return lax.all_to_all(mine, "ctx", 0, 0, tiled=True)


def scatter_sum(partial, ctx, tp):
    rows, width = partial.shape
    parts = partial.reshape(ctx, rows // ctx, tp, width // tp).transpose(0, 2, 1, 3)
    parts = parts.reshape(ctx * tp, rows // ctx, width // tp)
    return lax.psum_scatter(parts, ("ctx", "tp"), scatter_dimension=0, tiled=False)


def on_device(
    inputs,
    segments,
    gain_one,
    bias_one,
    gain_two,
    bias_two,
    w_qkv,
    b_qkv,
    w_out,
    out_bias,
    w_up,
    b_up,
    w_down,
    cotangent,
):
    f32, bf16 = jnp.float32, jnp.bfloat16
    dp, ctx, tp = lax.axis_size("dp"), lax.axis_size("ctx"), lax.axis_size("tp")
    my_ctx, my_tp = lax.axis_index("ctx"), lax.axis_index("tp")
    local_rows, width = inputs.shape[1:]
    length = local_rows * ctx
    share = width // tp
    owned = w_qkv.shape[0]
    heads = w_qkv.shape[2] // HD
    slots = -(-heads // ctx)
    head_width = slots * HD
    units = w_up.shape[1] // ctx
    pad_heads = slots * ctx * HD - heads * HD

    qkv_blocks = jnp.pad(w_qkv, ((0, 0), (0, 0), (0, pad_heads)))
    qkv_blocks = qkv_blocks.reshape(owned, 3, ctx, head_width).transpose(2, 0, 1, 3)
    out_blocks = jnp.pad(w_out, ((0, 0), (0, pad_heads))).reshape(owned, ctx, head_width)
    blocks = jnp.concatenate(
        [
            w_up.reshape(owned, ctx, units).transpose(1, 0, 2),
            w_down.reshape(owned, ctx, units).transpose(1, 0, 2),
            qkv_blocks.reshape(ctx, owned, 3 * head_width),
            out_blocks.transpose(1, 0, 2),
        ],
        axis=-1,
    )
    columns = weights_to_columns(blocks).reshape(width, -1)
    up = columns[:, :units]
    down = columns[:, units : 2 * units]
    qkv = columns[:, 2 * units : 2 * units + 3 * head_width]
    out = columns[:, 2 * units + 3 * head_width :]

    seg_columns = jnp.broadcast_to(segments[0].astype(bf16)[:, None], (local_rows, 128))
    packed = jnp.concatenate([inputs[0], cotangent[0], seg_columns], axis=-1)
    row = gather_tokens(packed)
    tokens = row[:, :width].astype(f32)
    grad_out = row[:, width : 2 * width]
    seg = row[:, 2 * width]

    qkv_bias = jnp.pad(b_qkv, ((0, 0), (0, pad_heads))).reshape(3, ctx, head_width)
    qkv_bias = lax.dynamic_index_in_dim(qkv_bias, my_ctx, 1, keepdims=False).reshape(-1)
    up_bias = lax.dynamic_slice_in_dim(b_up, my_ctx * units, units, 0)

    average = jnp.mean(tokens, axis=-1, keepdims=True)
    centered = tokens - average
    inverse = lax.rsqrt(jnp.mean(centered * centered, axis=-1, keepdims=True) + NORM_EPSILON)
    xhat = centered * inverse
    norm_one = (xhat * gain_one + bias_one).astype(bf16)
    norm_two = (xhat * gain_two + bias_two).astype(bf16)

    projected = dot_f32(norm_one, qkv) + qkv_bias
    cosine_table, sine_table = angle_tables(0, length)
    softmax_scale = 1.0 / math.sqrt(HD)
    position = jnp.arange(length)
    allowed = (position[None, :] <= position[:, None]) & (seg[None, :] == seg[:, None])
    kept = []
    for slot in range(slots):
        first = slot * HD
        query = rotate(projected[:, first : first + HD], cosine_table, sine_table).astype(bf16)
        first += head_width
        key = rotate(projected[:, first : first + HD], cosine_table, sine_table).astype(bf16)
        first += head_width
        value = projected[:, first : first + HD].astype(bf16)
        scores = jnp.where(allowed, dot_f32(query, key, LAST) * softmax_scale, NEG_LARGE)
        exponent = jnp.exp(scores - jnp.max(scores, axis=-1, keepdims=True))
        softmax = exponent / jnp.sum(exponent, axis=-1, keepdims=True)
        attended = dot_f32(softmax.astype(bf16), value)
        kept.append((query, key, value, softmax, attended))
    attended_low = jnp.concatenate([item[4] for item in kept], axis=-1).astype(bf16)

    pre_gelu = dot_f32(norm_two, up) + up_bias
    activated = jax.nn.gelu(pre_gelu, approximate=False).astype(bf16)
    branch = dot_f32(attended_low, out, LAST) + dot_f32(activated, down, LAST)
    branch_share = scatter_sum(branch.astype(bf16), ctx, tp).astype(f32)

    grad_attended = dot_f32(grad_out, out).astype(bf16)
    grad_activated = dot_f32(grad_out, down)
    gelu_pull = jax.vjp(lambda current: jax.nn.gelu(current, approximate=False), pre_gelu)[1]
    grad_pre = gelu_pull(grad_activated)[0].astype(bf16)
    grad_w_out = dot_f32(grad_out, attended_low, ROWS)
    grad_w_down = dot_f32(grad_out, activated, ROWS)
    grad_w_up = dot_f32(norm_two, grad_pre, ROWS)
    grad_b_up = jnp.sum(grad_pre.astype(f32), axis=0)
    grad_norm_two = dot_f32(grad_pre, up, LAST)

    pieces = ([], [], [])
    for slot, (query, key, value, softmax, attended) in enumerate(kept):
        grad_rows = grad_attended[:, slot * HD : (slot + 1) * HD]
        grad_dots = jnp.sum(grad_rows.astype(f32) * attended, axis=-1, keepdims=True)
        grad_probs = dot_f32(grad_rows, value, LAST)
        grad_scores = (softmax * (grad_probs - grad_dots)).astype(bf16)
        grad_query = dot_f32(grad_scores, key) * softmax_scale
        grad_key = dot_f32(grad_scores, query, ROWS) * softmax_scale
        pieces[0].append(rotate(grad_query, cosine_table, -sine_table))
        pieces[1].append(rotate(grad_key, cosine_table, -sine_table))
        pieces[2].append(dot_f32(softmax.astype(bf16), grad_rows, ROWS))
    grad_projected = jnp.concatenate(pieces[0] + pieces[1] + pieces[2], axis=-1).astype(bf16)
    grad_w_qkv = dot_f32(norm_one, grad_projected, ROWS)
    grad_b_qkv = jnp.sum(grad_projected.astype(f32), axis=0)
    grad_norm_one = dot_f32(grad_projected, qkv, LAST)

    grad_gain_one = jnp.sum(grad_norm_one * xhat, axis=0)
    grad_bias_one = jnp.sum(grad_norm_one, axis=0)
    grad_gain_two = jnp.sum(grad_norm_two * xhat, axis=0)
    grad_bias_two = jnp.sum(grad_norm_two, axis=0)
    pulled = grad_norm_one * gain_one + grad_norm_two * gain_two
    input_term = inverse * (
        pulled
        - jnp.mean(pulled, axis=-1, keepdims=True)
        - xhat * jnp.mean(pulled * xhat, axis=-1, keepdims=True)
    )
    input_share = scatter_sum(input_term.astype(bf16), ctx, tp).astype(f32)

    grads = jnp.concatenate([grad_w_up, grad_w_down, grad_w_qkv, grad_w_out], axis=-1)
    grads = grads.astype(bf16).reshape(dp, ctx, owned, -1)
    own = grads_to_owners(grads).astype(f32)
    own_up = own[:, :, :units].transpose(1, 0, 2).reshape(owned, -1)
    own_down = own[:, :, units : 2 * units].transpose(1, 0, 2).reshape(owned, -1)
    own_qkv = own[:, :, 2 * units : 2 * units + 3 * head_width]
    own_qkv = own_qkv.reshape(ctx, owned, 3, head_width).transpose(1, 2, 0, 3)
    own_qkv = own_qkv.reshape(owned, 3, ctx * head_width)[:, :, : heads * HD]
    own_out = own[:, :, 2 * units + 3 * head_width :].transpose(1, 0, 2)
    own_out = own_out.reshape(owned, -1)[:, : heads * HD]

    grad_bias = jnp.sum(cotangent[0].astype(f32), axis=0) * (my_tp == 0).astype(f32)
    place = (jnp.arange(tp)[:, None] == my_tp) & (jnp.arange(ctx)[None, :] == my_ctx)
    local = jnp.concatenate([grad_b_qkv, grad_b_up])
    spread = jnp.where(place[:, :, None], local, 0.0)
    total = lax.psum(
        jnp.concatenate(
            [
                grad_gain_one,
                grad_bias_one,
                grad_gain_two,
                grad_bias_two,
                grad_bias,
                spread.reshape(-1),
            ]
        ),
        ("dp", "ctx", "tp"),
    )
    spread = total[5 * width :].reshape(tp, ctx, -1)
    spread = lax.dynamic_index_in_dim(spread, my_tp, 0, keepdims=False)
    sum_b_qkv = spread[:, : 3 * head_width].reshape(ctx, 3, head_width).transpose(1, 0, 2)
    sum_b_qkv = sum_b_qkv.reshape(3, -1)[:, : heads * HD]
    sum_b_up = spread[:, 3 * head_width :].reshape(-1)

    start = my_tp * share
    token_share = lax.dynamic_slice_in_dim(inputs[0], start, share, 1).astype(f32)
    bias_share = lax.dynamic_slice_in_dim(out_bias, start, share, 0)
    cotangent_share = lax.dynamic_slice_in_dim(cotangent[0], start, share, 1).astype(f32)
    output = token_share + branch_share + bias_share
    grad_inputs = cotangent_share + input_share
    return (
        output[None],
        grad_inputs[None],
        total[:width],
        total[width : 2 * width],
        total[2 * width : 3 * width],
        total[3 * width : 4 * width],
        own_qkv,
        sum_b_qkv,
        own_out,
        total[4 * width : 5 * width],
        own_up,
        sum_b_up,
        own_down,
    )


def solution(mesh):
    return jax.shard_map(
        on_device,
        mesh=mesh,
        in_specs=(
            P("dp", "ctx", None),
            P("dp", "ctx"),
            P(),
            P(),
            P(),
            P(),
            P(("dp", "ctx"), None, "tp"),
            P(None, "tp"),
            P(("dp", "ctx"), "tp"),
            P(),
            P(("dp", "ctx"), "tp"),
            P("tp"),
            P(("dp", "ctx"), "tp"),
            P("dp", "ctx", None),
        ),
        out_specs=(
            P("dp", "ctx", "tp"),
            P("dp", "ctx", "tp"),
            P(),
            P(),
            P(),
            P(),
            P(("dp", "ctx"), None, "tp"),
            P(None, "tp"),
            P(("dp", "ctx"), "tp"),
            P(),
            P(("dp", "ctx"), "tp"),
            P("tp"),
            P(("dp", "ctx"), "tp"),
        ),
        check_vma=False,
    )
```

```python
import functools
import math

import jax
import jax.numpy as jnp
from jax import lax
from jax.experimental import pallas as pl
from jax.experimental.pallas import tpu as pltpu
from jax.sharding import PartitionSpec as P

HD = 64
ROT = 16

NORM_EPSILON = 1e-05
NEG_LARGE = -1e30
LAST = (((1,), (1,)), ((), ()))
ROWS = (((0,), (0,)), ((), ()))


def dot_f32(a, b, dims=(((1,), (0,)), ((), ()))):
    return lax.dot_general(a, b, dims, preferred_element_type=jnp.float32)


def angle_tables(first_row, length):
    positions = (first_row + jnp.arange(length)).astype(jnp.float32)
    frequency = 10000.0 ** (-(jnp.arange(ROT // 2).astype(jnp.float32) * 2.0 / ROT))
    angles = positions[:, None] * frequency[None, :]
    return (jnp.cos(angles), jnp.sin(angles))


def rotate(values, cosine_table, sine_table):
    half_rot = ROT // 2
    lower = values[..., :half_rot]
    upper = values[..., half_rot : 2 * half_rot]
    return jnp.concatenate(
        [
            lower * cosine_table - upper * sine_table,
            upper * cosine_table + lower * sine_table,
            values[..., 2 * half_rot :],
        ],
        axis=-1,
    )


MESH = pl.DeviceIdType.MESH
INNER = 2


def greet(ctx, dp, tp, my_ctx, my_dp, my_tp):
    barrier = pltpu.get_barrier_semaphore()
    for step in range(1, ctx):
        peer = {"ctx": lax.rem(my_ctx + step, ctx)}
        pl.semaphore_signal(barrier, inc=1, device_id=peer, device_id_type=MESH)
    for step in range(1, dp):
        peer = {"dp": lax.rem(my_dp + step, dp)}
        pl.semaphore_signal(barrier, inc=1, device_id=peer, device_id_type=MESH)
    for step in range(1, tp):
        peer = {"tp": lax.rem(my_tp + step, tp)}
        pl.semaphore_signal(barrier, inc=1, device_id=peer, device_id_type=MESH)
    pl.semaphore_wait(barrier, ctx + dp + tp - 3)


class Copies:
    def __init__(self, send_sems, recv_sems):
        self.send_sems, self.recv_sems, self.items = send_sems, recv_sems, []

    def start(self, src, dst, peer):
        place = len(self.items)
        copy = pltpu.make_async_remote_copy(
            src_ref=src,
            dst_ref=dst,
            send_sem=self.send_sems.at[place],
            recv_sem=self.recv_sems.at[place],
            device_id=peer,
            device_id_type=MESH,
        )
        copy.start()
        self.items.append(copy)
        return copy

    def finish(self):
        for copy in self.items:
            copy.wait_send()


def gather_kernel(
    ctx, dp, tp, packed, blocks, row, columns, send_sems, recv_sems, local_sems
):
    my_ctx, my_dp, my_tp = lax.axis_index("ctx"), lax.axis_index("dp"), lax.axis_index("tp")
    outer = ctx // INNER
    my_z, my_x = my_ctx // INNER, lax.rem(my_ctx, INNER)
    rows = packed.shape[0]
    half = rows // tp

    def piece(owner, core):
        return row.at[pl.ds(pl.multiple_of(owner * rows + core * half, half), half)]

    own_row = pltpu.make_async_copy(
        packed, row.at[pl.ds(pl.multiple_of(my_ctx * rows, rows), rows)], local_sems.at[0]
    )
    own_block = pltpu.make_async_copy(
        blocks.at[my_ctx], columns.at[my_dp, my_ctx], local_sems.at[1]
    )
    own_row.start()
    own_block.start()
    greet(ctx, dp, tp, my_ctx, my_dp, my_tp)
    copies = Copies(send_sems, recv_sems)
    mine = packed.at[pl.ds(pl.multiple_of(my_tp * half, half), half)]
    partner = {"ctx": my_z * INNER + (INNER - 1 - my_x)}
    sibling = {"tp": tp - 1 - my_tp}
    along = []
    for step in range(1, outer):
        target = lax.rem(my_z + step, outer) * INNER + my_x
        along.append(copies.start(mine, piece(my_ctx, my_tp), {"ctx": target}))
    across = [copies.start(mine, piece(my_ctx, my_tp), partner)]
    exchanged = []
    for step in range(1, ctx):
        target = lax.rem(my_ctx + step, ctx)
        exchanged.append(
            copies.start(blocks.at[target], columns.at[my_dp, my_ctx], {"ctx": target})
        )
    to_sibling = []
    for step in range(1, outer):
        source = lax.rem(my_z + outer - step, outer) * INNER + my_x
        along[step - 1].wait_recv()
        across.append(copies.start(piece(source, my_tp), piece(source, my_tp), partner))
        to_sibling.append(copies.start(piece(source, my_tp), piece(source, my_tp), sibling))
    over_dp = []
    for other in range(1, dp):
        target = {"dp": lax.rem(my_dp + other, dp)}
        over_dp.append(
            copies.start(blocks.at[my_ctx], columns.at[my_dp, my_ctx], target)
        )
    for step in range(1, ctx):
        source = lax.rem(my_ctx + ctx - step, ctx)
        exchanged[step - 1].wait_recv()
        for other in range(1, dp):
            target = {"dp": lax.rem(my_dp + other, dp)}
            over_dp.append(
                copies.start(columns.at[my_dp, source], columns.at[my_dp, source], target)
            )
    for step in range(outer):
        source = lax.rem(my_z + outer - step, outer) * INNER + (INNER - 1 - my_x)
        across[step].wait_recv()
        to_sibling.append(copies.start(piece(source, my_tp), piece(source, my_tp), sibling))
    for copy in over_dp + to_sibling:
        copy.wait_recv()
    copies.finish()
    own_row.wait()
    own_block.wait()


def gather_all(packed, blocks, dp, ctx, tp):
    outer = ctx // INNER
    count = (outer - 1) + outer + (ctx - 1) + (2 * outer - 1) + ctx * (dp - 1)
    return pl.pallas_call(
        functools.partial(gather_kernel, ctx, dp, tp),
        out_shape=(
            jax.ShapeDtypeStruct((ctx * packed.shape[0], packed.shape[1]), packed.dtype),
            jax.ShapeDtypeStruct((dp,) + blocks.shape, blocks.dtype),
        ),
        in_specs=[pl.BlockSpec(memory_space=pl.ANY)] * 2,
        out_specs=(pl.BlockSpec(memory_space=pl.ANY),) * 2,
        scratch_shapes=[
            pltpu.SemaphoreType.DMA((count,)),
            pltpu.SemaphoreType.DMA((count,)),
            pltpu.SemaphoreType.DMA((2,)),
        ],
        compiler_params=pltpu.CompilerParams(collective_id=0, has_side_effects=True),
    )(packed, blocks)


def reduce_kernel(
    ctx,
    dp,
    tp,
    partial,
    grads,
    vectors,
    sums,
    own_grads,
    totals,
    from_core,
    to_x,
    from_x,
    to_z,
    from_z,
    from_y,
    summed,
    core_vector,
    x_vector,
    passed_vector,
    z_vectors,
    y_vectors,
    send_sems,
    recv_sems,
    local_sem,
):
    f32, bf16 = jnp.float32, jnp.bfloat16
    my_ctx, my_dp, my_tp = lax.axis_index("ctx"), lax.axis_index("dp"), lax.axis_index("tp")
    outer = ctx // INNER
    my_z, my_x = my_ctx // INNER, lax.rem(my_ctx, INNER)
    rows = sums.shape[0]
    greet(ctx, dp, tp, my_ctx, my_dp, my_tp)
    copies = Copies(send_sems, recv_sems)
    partner = {"ctx": my_z * INNER + (INNER - 1 - my_x)}
    sibling = {"tp": tp - 1 - my_tp}
    other_core = tp - 1 - my_tp

    def group(step):
        first = lax.rem(my_z + step, outer) * INNER * rows
        return pl.ds(pl.multiple_of(first, rows), INNER * rows)

    def token_rows(step, x):
        first = (lax.rem(my_z + step, outer) * INNER + x) * rows
        return pl.ds(pl.multiple_of(first, rows), rows)

    vector_core = copies.start(vectors, core_vector, sibling)
    order = list(range(1, outer)) + [0]
    over_core = {}
    for step in order:
        here = group(step)
        over_core[step] = copies.start(
            partial.at[other_core, here], from_core.at[here], sibling
        )
    over_y = []
    for other in range(1, dp):
        target = lax.rem(my_dp + other, dp)
        over_y.append(copies.start(grads.at[target], from_y.at[other - 1], {"dp": target}))

    over_x = {}
    for step in order:
        over_core[step].wait_recv()
        there = token_rows(step, INNER - 1 - my_x)
        to_x[step] = (
            partial[my_tp, there, :].astype(f32) + from_core[there, :].astype(f32)
        ).astype(bf16)
        over_x[step] = copies.start(to_x.at[step], from_x.at[step], partner)

    vector_core.wait_recv()
    passed_vector[0] = vectors[...] + core_vector[...]
    vector_x = copies.start(passed_vector.at[0], x_vector, partner)

    def own_sum(step):
        here = token_rows(step, my_x)
        local = partial[my_tp, here, :].astype(f32) + from_core[here, :].astype(f32)
        return local + from_x[step].astype(f32)

    over_z = {}
    for step in range(1, outer):
        over_x[step].wait_recv()
        to_z[step - 1] = own_sum(step).astype(bf16)
        target = lax.rem(my_z + step, outer) * INNER + my_x
        over_z[step] = copies.start(to_z.at[step - 1], from_z.at[step - 1], {"ctx": target})

    vector_x.wait_recv()
    passed_vector[1] = passed_vector[0] + x_vector[...]
    z_vectors[my_z] = passed_vector[1]
    vector_z = []
    for step in range(1, outer):
        target = lax.rem(my_z + step, outer) * INNER + my_x
        vector_z.append(
            copies.start(passed_vector.at[1], z_vectors.at[my_z], {"ctx": target})
        )

    for copy in over_y:
        copy.wait_recv()
    over_ctx = []
    for step in list(range(1, ctx)) + [0]:
        target = lax.rem(my_ctx + step, ctx)
        total = grads[my_dp, target].astype(f32)
        for other in range(1, dp):
            total = total + from_y[other - 1, target].astype(f32)
        summed[step] = total.astype(bf16)
        if step > 0:
            over_ctx.append(
                copies.start(summed.at[step], own_grads.at[my_ctx], {"ctx": target})
            )
    own = pltpu.make_async_copy(summed.at[0], own_grads.at[my_ctx], local_sem)
    own.start()

    for copy in vector_z:
        copy.wait_recv()
    total = z_vectors[0]
    for place in range(1, outer):
        total = total + z_vectors[place]
    passed_vector[2] = total
    y_vectors[my_dp] = total
    vector_y = []
    for other in range(1, dp):
        target = {"dp": lax.rem(my_dp + other, dp)}
        vector_y.append(copies.start(passed_vector.at[2], y_vectors.at[my_dp], target))

    over_x[0].wait_recv()
    result = own_sum(0)
    for step in range(1, outer):
        over_z[step].wait_recv()
        result = result + from_z[step - 1].astype(f32)
    sums[...] = result
    for copy in vector_y:
        copy.wait_recv()
    total = y_vectors[0]
    for place in range(1, dp):
        total = total + y_vectors[place]
    totals[...] = total
    for copy in over_ctx:
        copy.wait_recv()
    copies.finish()
    own.wait()


def reduce_all(partial, grads, vectors, dp, ctx, tp):
    outer = ctx // INNER
    rows, width = partial.shape[1] // ctx, partial.shape[2]
    block = grads.shape[2:]
    bf16 = jnp.bfloat16
    count = outer + (dp - 1) + outer + (outer - 1) + (ctx - 1)
    count += 2 + (outer - 1) + (dp - 1)
    vmem = pl.BlockSpec(memory_space=pltpu.VMEM)
    return pl.pallas_call(
        functools.partial(reduce_kernel, ctx, dp, tp),
        out_shape=(
            jax.ShapeDtypeStruct((rows, width), jnp.float32),
            jax.ShapeDtypeStruct((ctx,) + block, bf16),
            jax.ShapeDtypeStruct(vectors.shape, jnp.float32),
        ),
        in_specs=[vmem] * 3,
        out_specs=(vmem, pl.BlockSpec(memory_space=pl.ANY), vmem),
        scratch_shapes=[
            pltpu.VMEM(partial.shape[1:], bf16),
            pltpu.VMEM((outer, rows, width), bf16),
            pltpu.VMEM((outer, rows, width), bf16),
            pltpu.VMEM((outer - 1, rows, width), bf16),
            pltpu.VMEM((outer - 1, rows, width), bf16),
            pltpu.VMEM((dp - 1, ctx) + block, bf16),
            pltpu.VMEM((ctx,) + block, bf16),
            pltpu.VMEM(vectors.shape, jnp.float32),
            pltpu.VMEM(vectors.shape, jnp.float32),
            pltpu.VMEM((3,) + vectors.shape, jnp.float32),
            pltpu.VMEM((outer,) + vectors.shape, jnp.float32),
            pltpu.VMEM((dp,) + vectors.shape, jnp.float32),
            pltpu.SemaphoreType.DMA((count,)),
            pltpu.SemaphoreType.DMA((count,)),
            pltpu.SemaphoreType.DMA,
        ],
        compiler_params=pltpu.CompilerParams(
            collective_id=1, has_side_effects=True, vmem_limit_bytes=48 * 2**20
        ),
    )(partial, grads, vectors)


def on_device(
    inputs,
    segments,
    gain_one,
    bias_one,
    gain_two,
    bias_two,
    w_qkv,
    b_qkv,
    w_out,
    out_bias,
    w_up,
    b_up,
    w_down,
    cotangent,
):
    f32, bf16 = jnp.float32, jnp.bfloat16
    dp, ctx, tp = lax.axis_size("dp"), lax.axis_size("ctx"), lax.axis_size("tp")
    my_ctx, my_tp = lax.axis_index("ctx"), lax.axis_index("tp")
    local_rows, width = inputs.shape[1:]
    length = local_rows * ctx
    share = width // tp
    owned = w_qkv.shape[0]
    heads = w_qkv.shape[2] // HD
    slots = -(-heads // ctx)
    head_width = slots * HD
    units = w_up.shape[1] // ctx
    pad_heads = slots * ctx * HD - heads * HD

    qkv_blocks = jnp.pad(w_qkv, ((0, 0), (0, 0), (0, pad_heads)))
    qkv_blocks = qkv_blocks.reshape(owned, 3, ctx, head_width).transpose(2, 0, 1, 3)
    out_blocks = jnp.pad(w_out, ((0, 0), (0, pad_heads))).reshape(owned, ctx, head_width)
    blocks = jnp.concatenate(
        [
            w_up.reshape(owned, ctx, units).transpose(1, 0, 2),
            w_down.reshape(owned, ctx, units).transpose(1, 0, 2),
            qkv_blocks.reshape(ctx, owned, 3 * head_width),
            out_blocks.transpose(1, 0, 2),
        ],
        axis=-1,
    )
    block_width = blocks.shape[-1]
    pad_rows, pad_width = -owned % 16, -block_width % 128
    blocks = jnp.pad(blocks, ((0, 0), (0, pad_rows), (0, pad_width)))
    seg_columns = jnp.broadcast_to(segments[0].astype(bf16)[:, None], (local_rows, 128))
    packed = jnp.concatenate([inputs[0], cotangent[0], seg_columns], axis=-1)
    row, columns = gather_all(packed, blocks, dp, ctx, tp)
    columns = columns[:, :, :owned, :block_width].reshape(width, -1)
    up = columns[:, :units]
    down = columns[:, units : 2 * units]
    qkv = columns[:, 2 * units : 2 * units + 3 * head_width]
    out = columns[:, 2 * units + 3 * head_width :]

    tokens = row[:, :width].astype(f32)
    grad_out = row[:, width : 2 * width]
    seg = row[:, 2 * width]

    qkv_bias = jnp.pad(b_qkv, ((0, 0), (0, pad_heads))).reshape(3, ctx, head_width)
    qkv_bias = lax.dynamic_index_in_dim(qkv_bias, my_ctx, 1, keepdims=False).reshape(-1)
    up_bias = lax.dynamic_slice_in_dim(b_up, my_ctx * units, units, 0)

    average = jnp.mean(tokens, axis=-1, keepdims=True)
    centered = tokens - average
    inverse = lax.rsqrt(jnp.mean(centered * centered, axis=-1, keepdims=True) + NORM_EPSILON)
    xhat = centered * inverse
    norm_one = (xhat * gain_one + bias_one).astype(bf16)
    norm_two = (xhat * gain_two + bias_two).astype(bf16)

    projected = dot_f32(norm_one, qkv) + qkv_bias
    cosine_table, sine_table = angle_tables(0, length)
    softmax_scale = 1.0 / math.sqrt(HD)
    position = jnp.arange(length)
    allowed = (position[None, :] <= position[:, None]) & (seg[None, :] == seg[:, None])
    kept = []
    for slot in range(slots):
        first = slot * HD
        query = rotate(projected[:, first : first + HD], cosine_table, sine_table).astype(bf16)
        first += head_width
        key = rotate(projected[:, first : first + HD], cosine_table, sine_table).astype(bf16)
        first += head_width
        value = projected[:, first : first + HD].astype(bf16)
        scores = jnp.where(allowed, dot_f32(query, key, LAST) * softmax_scale, NEG_LARGE)
        exponent = jnp.exp(scores - jnp.max(scores, axis=-1, keepdims=True))
        softmax = exponent / jnp.sum(exponent, axis=-1, keepdims=True)
        attended = dot_f32(softmax.astype(bf16), value)
        kept.append((query, key, value, softmax, attended))
    attended_low = jnp.concatenate([item[4] for item in kept], axis=-1).astype(bf16)

    pre_gelu = dot_f32(norm_two, up) + up_bias
    activated = jax.nn.gelu(pre_gelu, approximate=False).astype(bf16)
    branch = dot_f32(attended_low, out, LAST) + dot_f32(activated, down, LAST)

    grad_attended = dot_f32(grad_out, out).astype(bf16)
    grad_activated = dot_f32(grad_out, down)
    gelu_pull = jax.vjp(lambda current: jax.nn.gelu(current, approximate=False), pre_gelu)[1]
    grad_pre = gelu_pull(grad_activated)[0].astype(bf16)
    grad_w_out = dot_f32(grad_out, attended_low, ROWS)
    grad_w_down = dot_f32(grad_out, activated, ROWS)
    grad_w_up = dot_f32(norm_two, grad_pre, ROWS)
    grad_b_up = jnp.sum(grad_pre.astype(f32), axis=0)
    grad_norm_two = dot_f32(grad_pre, up, LAST)

    pieces = ([], [], [])
    for slot, (query, key, value, softmax, attended) in enumerate(kept):
        grad_rows = grad_attended[:, slot * HD : (slot + 1) * HD]
        grad_dots = jnp.sum(grad_rows.astype(f32) * attended, axis=-1, keepdims=True)
        grad_probs = dot_f32(grad_rows, value, LAST)
        grad_scores = (softmax * (grad_probs - grad_dots)).astype(bf16)
        grad_query = dot_f32(grad_scores, key) * softmax_scale
        grad_key = dot_f32(grad_scores, query, ROWS) * softmax_scale
        pieces[0].append(rotate(grad_query, cosine_table, -sine_table))
        pieces[1].append(rotate(grad_key, cosine_table, -sine_table))
        pieces[2].append(dot_f32(softmax.astype(bf16), grad_rows, ROWS))
    grad_projected = jnp.concatenate(pieces[0] + pieces[1] + pieces[2], axis=-1).astype(bf16)
    grad_w_qkv = dot_f32(norm_one, grad_projected, ROWS)
    grad_b_qkv = jnp.sum(grad_projected.astype(f32), axis=0)
    grad_norm_one = dot_f32(grad_projected, qkv, LAST)

    grad_gain_one = jnp.sum(grad_norm_one * xhat, axis=0)
    grad_bias_one = jnp.sum(grad_norm_one, axis=0)
    grad_gain_two = jnp.sum(grad_norm_two * xhat, axis=0)
    grad_bias_two = jnp.sum(grad_norm_two, axis=0)
    pulled = grad_norm_one * gain_one + grad_norm_two * gain_two
    input_term = inverse * (
        pulled
        - jnp.mean(pulled, axis=-1, keepdims=True)
        - xhat * jnp.mean(pulled * xhat, axis=-1, keepdims=True)
    )

    grads = jnp.concatenate([grad_w_up, grad_w_down, grad_w_qkv, grad_w_out], axis=-1)
    grads = grads.astype(bf16).reshape(dp, ctx, owned, -1)
    grads = jnp.pad(grads, ((0, 0), (0, 0), (0, pad_rows), (0, pad_width)))

    grad_bias = jnp.sum(cotangent[0].astype(f32), axis=0) * (my_tp == 0).astype(f32)
    place = (jnp.arange(tp)[:, None] == my_tp) & (jnp.arange(ctx)[None, :] == my_ctx)
    local = jnp.concatenate([grad_b_qkv, grad_b_up])
    spread = jnp.where(place[:, :, None], local, 0.0)
    vectors = jnp.concatenate(
        [
            grad_gain_one,
            grad_bias_one,
            grad_gain_two,
            grad_bias_two,
            grad_bias,
            spread.reshape(-1),
        ]
    )
    vector_size = vectors.shape[0]
    vectors = jnp.pad(vectors, (0, -vector_size % 1024)).reshape(-1, 128)
    branch_low, input_low = branch.astype(bf16), input_term.astype(bf16)
    partial = jnp.stack(
        [
            jnp.concatenate(
                [
                    branch_low[:, part * share : (part + 1) * share],
                    input_low[:, part * share : (part + 1) * share],
                ],
                axis=-1,
            )
            for part in range(tp)
        ]
    )
    sums, own, total = reduce_all(partial, grads, vectors, dp, ctx, tp)
    branch_share, input_share = sums[:, :share], sums[:, share:]
    own = own[:, :owned, :block_width].astype(f32)
    own_up = own[:, :, :units].transpose(1, 0, 2).reshape(owned, -1)
    own_down = own[:, :, units : 2 * units].transpose(1, 0, 2).reshape(owned, -1)
    own_qkv = own[:, :, 2 * units : 2 * units + 3 * head_width]
    own_qkv = own_qkv.reshape(ctx, owned, 3, head_width).transpose(1, 2, 0, 3)
    own_qkv = own_qkv.reshape(owned, 3, ctx * head_width)[:, :, : heads * HD]
    own_out = own[:, :, 2 * units + 3 * head_width :].transpose(1, 0, 2)
    own_out = own_out.reshape(owned, -1)[:, : heads * HD]
    total = total.reshape(-1)[:vector_size]
    spread = total[5 * width :].reshape(tp, ctx, -1)
    spread = lax.dynamic_index_in_dim(spread, my_tp, 0, keepdims=False)
    sum_b_qkv = spread[:, : 3 * head_width].reshape(ctx, 3, head_width).transpose(1, 0, 2)
    sum_b_qkv = sum_b_qkv.reshape(3, -1)[:, : heads * HD]
    sum_b_up = spread[:, 3 * head_width :].reshape(-1)

    start = my_tp * share
    token_share = lax.dynamic_slice_in_dim(inputs[0], start, share, 1).astype(f32)
    bias_share = lax.dynamic_slice_in_dim(out_bias, start, share, 0)
    cotangent_share = lax.dynamic_slice_in_dim(cotangent[0], start, share, 1).astype(f32)
    output = token_share + branch_share + bias_share
    grad_inputs = cotangent_share + input_share
    return (
        output[None],
        grad_inputs[None],
        total[:width],
        total[width : 2 * width],
        total[2 * width : 3 * width],
        total[3 * width : 4 * width],
        own_qkv,
        sum_b_qkv,
        own_out,
        total[4 * width : 5 * width],
        own_up,
        sum_b_up,
        own_down,
    )


def solution(mesh):
    return jax.shard_map(
        on_device,
        mesh=mesh,
        in_specs=(
            P("dp", "ctx", None),
            P("dp", "ctx"),
            P(),
            P(),
            P(),
            P(),
            P(("dp", "ctx"), None, "tp"),
            P(None, "tp"),
            P(("dp", "ctx"), "tp"),
            P(),
            P(("dp", "ctx"), "tp"),
            P("tp"),
            P(("dp", "ctx"), "tp"),
            P("dp", "ctx", None),
        ),
        out_specs=(
            P("dp", "ctx", "tp"),
            P("dp", "ctx", "tp"),
            P(),
            P(),
            P(),
            P(),
            P(("dp", "ctx"), None, "tp"),
            P(None, "tp"),
            P(("dp", "ctx"), "tp"),
            P(),
            P(("dp", "ctx"), "tp"),
            P("tp"),
            P(("dp", "ctx"), "tp"),
        ),
        check_vma=False,
    )
```

```python
import functools
import math

import jax
import jax.numpy as jnp
from jax import lax
from jax.experimental import pallas as pl
from jax.experimental.pallas import tpu as pltpu
from jax.sharding import PartitionSpec as P

HD = 64
ROT = 16

NORM_EPSILON = 1e-05
NEG_LARGE = -1e30
LAST = (((1,), (1,)), ((), ()))
ROWS = (((0,), (0,)), ((), ()))


def dot_f32(a, b, dims=(((1,), (0,)), ((), ()))):
    return lax.dot_general(a, b, dims, preferred_element_type=jnp.float32)


def angle_tables(first_row, length):
    positions = (first_row + jnp.arange(length)).astype(jnp.float32)
    frequency = 10000.0 ** (-(jnp.arange(ROT // 2).astype(jnp.float32) * 2.0 / ROT))
    angles = positions[:, None] * frequency[None, :]
    return (jnp.cos(angles), jnp.sin(angles))


def swap_matrix(size):
    source = lax.broadcasted_iota(jnp.int32, (size, size), 0)
    target = lax.broadcasted_iota(jnp.int32, (size, size), 1)
    dim = lax.rem(target, HD)
    half_rot = ROT // 2
    minus = (dim < half_rot) & (source == target + half_rot)
    plus = (dim >= half_rot) & (dim < ROT) & (source == target - half_rot)
    return jnp.where(plus, 1.0, 0.0) - jnp.where(minus, 1.0, 0.0)


def swapped(values, matrix):
    return lax.dot_general(
        values,
        matrix,
        (((1,), (0,)), ((), ())),
        preferred_element_type=jnp.float32,
        precision=lax.Precision.HIGHEST,
    )


def compute_kernel(
    width,
    units,
    share,
    row,
    columns,
    cosines,
    sines,
    norms,
    up_bias,
    qkv_bias,
    partial,
    grads,
    norm_grads,
    grad_b_up,
    grad_b_qkv,
    xhats,
    inverses,
    norm_one,
    norm_two,
    queries,
    keys,
    values,
    mixed,
    grad_attended,
    grad_pre,
    grad_query,
    grad_key,
    grad_value,
    grad_projected,
    hot,
):
    f32, bf16 = jnp.float32, jnp.bfloat16
    length = row.shape[0]
    tile = math.gcd(length, 256)
    tiles = length // tile
    both = units + HD
    scale = 1.0 / math.sqrt(HD)
    matrix = swap_matrix(2 * HD)
    norm_grads[...] = jnp.zeros_like(norm_grads)
    grad_b_up[...] = jnp.zeros_like(grad_b_up)
    grad_b_qkv[...] = jnp.zeros_like(grad_b_qkv)
    grad_key[...] = jnp.zeros_like(grad_key)
    grad_value[...] = jnp.zeros_like(grad_value)

    def first_pass(step, carry):
        here = pl.ds(pl.multiple_of(step * tile, tile), tile)
        tokens = row[here, :width].astype(f32)
        centered = tokens - jnp.mean(tokens, axis=-1, keepdims=True)
        variance = jnp.mean(centered * centered, axis=-1, keepdims=True)
        inverse = lax.rsqrt(variance + NORM_EPSILON)
        xhat = centered * inverse
        xhats[here, :] = xhat
        inverses[here, :] = inverse
        one = (xhat * norms[0:1, :] + norms[1:2, :]).astype(bf16)
        two = (xhat * norms[2:3, :] + norms[3:4, :]).astype(bf16)
        norm_one[here, :] = one
        norm_two[here, :] = two
        projected = dot_f32(one, columns[:, both + units :]) + qkv_bias[...]
        turning = projected[:, : 2 * HD]
        turned = turning * cosines[here, :] + swapped(turning, matrix) * sines[here, :]
        queries[here, :] = (turned[:, :HD].astype(bf16).astype(f32) * scale).astype(bf16)
        keys[here, :] = turned[:, HD:].astype(bf16)
        values[here, :] = projected[:, 2 * HD :].astype(bf16)
        lane = lax.broadcasted_iota(jnp.int32, (tile, 128), 1).astype(f32)
        segment = row[here, 2 * width :].astype(f32)
        hot[here, :] = jnp.where(segment == lane, 1.0, 0.0).astype(bf16)
        pre = dot_f32(two, columns[:, both : both + units]) + up_bias[...]
        cumulative = 0.5 * (1.0 + lax.erf(pre * math.sqrt(0.5)))
        density = jnp.exp(pre * pre * -0.5) * (1.0 / math.sqrt(2.0 * math.pi))
        mixed[here, :units] = (pre * cumulative).astype(bf16)
        grad_mixed = dot_f32(row[here, width : 2 * width], columns[:, :both])
        slope = (grad_mixed[:, :units] * (cumulative + pre * density)).astype(bf16)
        grad_pre[here, :] = slope
        grad_b_up[...] += jnp.sum(slope.astype(f32), axis=0, keepdims=True)
        grad_attended[here, :] = grad_mixed[:, units:].astype(bf16)
        return carry

    lax.fori_loop(0, tiles, first_pass, 0)

    for step in range(tiles):
        here = pl.ds(step * tile, tile)
        seen = (step + 1) * tile
        query, key, value = queries[here, :], keys[:seen, :], values[:seen, :]
        scores = dot_f32(query, key, LAST)
        same = dot_f32(hot[here, :], hot[:seen, :], LAST) > 0.5
        at_query = lax.broadcasted_iota(jnp.int32, (tile, seen), 0) + step * tile
        at_key = lax.broadcasted_iota(jnp.int32, (tile, seen), 1)
        scores = jnp.where(same & (at_key <= at_query), scores, NEG_LARGE)
        exponent = jnp.exp(scores - jnp.max(scores, axis=-1, keepdims=True))
        softmax = exponent / jnp.sum(exponent, axis=-1, keepdims=True)
        softmax_low = softmax.astype(bf16)
        attended = dot_f32(softmax_low, value)
        mixed[here, units:] = attended.astype(bf16)
        grad_rows = grad_attended[here, :]
        grad_dots = jnp.sum(grad_rows.astype(f32) * attended, axis=-1, keepdims=True)
        grad_probs = dot_f32(grad_rows, value, LAST)
        grad_scores = (softmax * (grad_probs - grad_dots)).astype(bf16)
        grad_query[here, :] = dot_f32(grad_scores, key) * scale
        grad_key[:, :seen] += dot_f32(query, grad_scores, ROWS)
        grad_value[:, :seen] += dot_f32(grad_rows, softmax_low, ROWS)

    for step in range(tiles):
        here = pl.ds(step * tile, tile)
        key_rows = grad_key[:, step * tile : (step + 1) * tile].T
        value_rows = grad_value[:, step * tile : (step + 1) * tile].T
        turning = jnp.concatenate([grad_query[here, :], key_rows], axis=-1)
        turned = turning * cosines[here, :] - swapped(turning, matrix) * sines[here, :]
        pulled = jnp.concatenate([turned, value_rows], axis=-1).astype(bf16)
        grad_projected[here, :] = pulled
        grad_b_qkv[...] += jnp.sum(pulled.astype(f32), axis=0, keepdims=True)

    def last_pass(step, carry):
        here = pl.ds(pl.multiple_of(step * tile, tile), tile)
        branch = dot_f32(mixed[here, :], columns[:, :both], LAST).astype(bf16)
        for part in range(width // share):
            partial[part, here, :share] = branch[:, part * share : (part + 1) * share]
        xhat = xhats[here, :]
        grad_one = dot_f32(grad_projected[here, :], columns[:, both + units :], LAST)
        grad_two = dot_f32(grad_pre[here, :], columns[:, both : both + units], LAST)
        norm_grads[0:1, :] += jnp.sum(grad_one * xhat, axis=0, keepdims=True)
        norm_grads[1:2, :] += jnp.sum(grad_one, axis=0, keepdims=True)
        norm_grads[2:3, :] += jnp.sum(grad_two * xhat, axis=0, keepdims=True)
        norm_grads[3:4, :] += jnp.sum(grad_two, axis=0, keepdims=True)
        pulled = grad_one * norms[0:1, :] + grad_two * norms[2:3, :]
        term = inverses[here, :] * (
            pulled
            - jnp.mean(pulled, axis=-1, keepdims=True)
            - xhat * jnp.mean(pulled * xhat, axis=-1, keepdims=True)
        )
        term = term.astype(bf16)
        for part in range(width // share):
            partial[part, here, share:] = term[:, part * share : (part + 1) * share]
        return carry

    lax.fori_loop(0, tiles, last_pass, 0)

    chunk = math.gcd(width, 256)
    for first in range(0, width, chunk):
        here = pl.ds(first, chunk)
        cotangents = row[:, width + first : width + first + chunk]
        grads[here, :both] = dot_f32(cotangents, mixed[...], ROWS).astype(bf16)
        up_grads = dot_f32(norm_two[:, here], grad_pre[...], ROWS).astype(bf16)
        grads[here, both : both + units] = up_grads
        qkv_grads = dot_f32(norm_one[:, here], grad_projected[...], ROWS).astype(bf16)
        grads[here, both + units :] = qkv_grads


def compute_all(row, columns, cosines, sines, norms, up_bias, qkv_bias, width, units, share):
    f32, bf16 = jnp.float32, jnp.bfloat16
    length = row.shape[0]
    vmem = pl.BlockSpec(memory_space=pltpu.VMEM)
    return pl.pallas_call(
        functools.partial(compute_kernel, width, units, share),
        out_shape=(
            jax.ShapeDtypeStruct((width // share, length, 2 * share), bf16),
            jax.ShapeDtypeStruct(columns.shape, bf16),
            jax.ShapeDtypeStruct((4, width), f32),
            jax.ShapeDtypeStruct((1, units), f32),
            jax.ShapeDtypeStruct((1, 3 * HD), f32),
        ),
        in_specs=[vmem] * 7,
        out_specs=(vmem,) * 5,
        scratch_shapes=[
            pltpu.VMEM((length, width), f32),
            pltpu.VMEM((length, 1), f32),
            pltpu.VMEM((length, width), bf16),
            pltpu.VMEM((length, width), bf16),
            pltpu.VMEM((length, HD), bf16),
            pltpu.VMEM((length, HD), bf16),
            pltpu.VMEM((length, HD), bf16),
            pltpu.VMEM((length, units + HD), bf16),
            pltpu.VMEM((length, HD), bf16),
            pltpu.VMEM((length, units), bf16),
            pltpu.VMEM((length, HD), f32),
            pltpu.VMEM((HD, length), f32),
            pltpu.VMEM((HD, length), f32),
            pltpu.VMEM((length, 3 * HD), bf16),
            pltpu.VMEM((length, 128), bf16),
        ],
        compiler_params=pltpu.CompilerParams(vmem_limit_bytes=56 * 2**20),
    )(row, columns, cosines, sines, norms, up_bias, qkv_bias)


MESH = pl.DeviceIdType.MESH
INNER = 2


def greet(ctx, dp, tp, my_ctx, my_dp, my_tp):
    barrier = pltpu.get_barrier_semaphore()
    for step in range(1, ctx):
        peer = {"ctx": lax.rem(my_ctx + step, ctx)}
        pl.semaphore_signal(barrier, inc=1, device_id=peer, device_id_type=MESH)
    for step in range(1, dp):
        peer = {"dp": lax.rem(my_dp + step, dp)}
        pl.semaphore_signal(barrier, inc=1, device_id=peer, device_id_type=MESH)
    for step in range(1, tp):
        peer = {"tp": lax.rem(my_tp + step, tp)}
        pl.semaphore_signal(barrier, inc=1, device_id=peer, device_id_type=MESH)
    pl.semaphore_wait(barrier, ctx + dp + tp - 3)


class Copies:
    def __init__(self, send_sems, recv_sems):
        self.send_sems, self.recv_sems, self.items = send_sems, recv_sems, []

    def start(self, src, dst, peer):
        place = len(self.items)
        copy = pltpu.make_async_remote_copy(
            src_ref=src,
            dst_ref=dst,
            send_sem=self.send_sems.at[place],
            recv_sem=self.recv_sems.at[place],
            device_id=peer,
            device_id_type=MESH,
        )
        copy.start()
        self.items.append(copy)
        return copy

    def finish(self):
        for copy in self.items:
            copy.wait_send()


def gather_kernel(
    ctx, dp, tp, packed, blocks, row, columns, send_sems, recv_sems, local_sems
):
    my_ctx, my_dp, my_tp = lax.axis_index("ctx"), lax.axis_index("dp"), lax.axis_index("tp")
    outer = ctx // INNER
    my_z, my_x = my_ctx // INNER, lax.rem(my_ctx, INNER)
    rows = packed.shape[0]
    half = rows // tp

    def piece(owner, core):
        return row.at[pl.ds(pl.multiple_of(owner * rows + core * half, half), half)]

    own_row = pltpu.make_async_copy(
        packed, row.at[pl.ds(pl.multiple_of(my_ctx * rows, rows), rows)], local_sems.at[0]
    )
    own_block = pltpu.make_async_copy(
        blocks.at[my_ctx], columns.at[my_dp, my_ctx], local_sems.at[1]
    )
    own_row.start()
    own_block.start()
    greet(ctx, dp, tp, my_ctx, my_dp, my_tp)
    copies = Copies(send_sems, recv_sems)
    mine = packed.at[pl.ds(pl.multiple_of(my_tp * half, half), half)]
    partner = {"ctx": my_z * INNER + (INNER - 1 - my_x)}
    sibling = {"tp": tp - 1 - my_tp}
    along = []
    for step in range(1, outer):
        target = lax.rem(my_z + step, outer) * INNER + my_x
        along.append(copies.start(mine, piece(my_ctx, my_tp), {"ctx": target}))
    across = [copies.start(mine, piece(my_ctx, my_tp), partner)]
    exchanged = []
    for step in range(1, ctx):
        target = lax.rem(my_ctx + step, ctx)
        exchanged.append(
            copies.start(blocks.at[target], columns.at[my_dp, my_ctx], {"ctx": target})
        )
    to_sibling = []
    for step in range(1, outer):
        source = lax.rem(my_z + outer - step, outer) * INNER + my_x
        along[step - 1].wait_recv()
        across.append(copies.start(piece(source, my_tp), piece(source, my_tp), partner))
        to_sibling.append(copies.start(piece(source, my_tp), piece(source, my_tp), sibling))
    over_dp = []
    for other in range(1, dp):
        target = {"dp": lax.rem(my_dp + other, dp)}
        over_dp.append(
            copies.start(blocks.at[my_ctx], columns.at[my_dp, my_ctx], target)
        )
    for step in range(1, ctx):
        source = lax.rem(my_ctx + ctx - step, ctx)
        exchanged[step - 1].wait_recv()
        for other in range(1, dp):
            target = {"dp": lax.rem(my_dp + other, dp)}
            over_dp.append(
                copies.start(columns.at[my_dp, source], columns.at[my_dp, source], target)
            )
    for step in range(outer):
        source = lax.rem(my_z + outer - step, outer) * INNER + (INNER - 1 - my_x)
        across[step].wait_recv()
        to_sibling.append(copies.start(piece(source, my_tp), piece(source, my_tp), sibling))
    for copy in over_dp + to_sibling:
        copy.wait_recv()
    copies.finish()
    own_row.wait()
    own_block.wait()


def gather_all(packed, blocks, dp, ctx, tp):
    outer = ctx // INNER
    count = (outer - 1) + outer + (ctx - 1) + (2 * outer - 1) + ctx * (dp - 1)
    return pl.pallas_call(
        functools.partial(gather_kernel, ctx, dp, tp),
        out_shape=(
            jax.ShapeDtypeStruct((ctx * packed.shape[0], packed.shape[1]), packed.dtype),
            jax.ShapeDtypeStruct((dp,) + blocks.shape, blocks.dtype),
        ),
        in_specs=[pl.BlockSpec(memory_space=pl.ANY)] * 2,
        out_specs=(pl.BlockSpec(memory_space=pl.ANY),) * 2,
        scratch_shapes=[
            pltpu.SemaphoreType.DMA((count,)),
            pltpu.SemaphoreType.DMA((count,)),
            pltpu.SemaphoreType.DMA((2,)),
        ],
        compiler_params=pltpu.CompilerParams(collective_id=0, has_side_effects=True),
    )(packed, blocks)


def reduce_kernel(
    ctx,
    dp,
    tp,
    partial,
    grads,
    vectors,
    sums,
    own_grads,
    totals,
    from_core,
    to_x,
    from_x,
    to_z,
    from_z,
    from_y,
    summed,
    core_vector,
    x_vector,
    passed_vector,
    z_vectors,
    y_vectors,
    send_sems,
    recv_sems,
    local_sem,
):
    f32, bf16 = jnp.float32, jnp.bfloat16
    my_ctx, my_dp, my_tp = lax.axis_index("ctx"), lax.axis_index("dp"), lax.axis_index("tp")
    outer = ctx // INNER
    my_z, my_x = my_ctx // INNER, lax.rem(my_ctx, INNER)
    rows = sums.shape[0]
    greet(ctx, dp, tp, my_ctx, my_dp, my_tp)
    copies = Copies(send_sems, recv_sems)
    partner = {"ctx": my_z * INNER + (INNER - 1 - my_x)}
    sibling = {"tp": tp - 1 - my_tp}
    other_core = tp - 1 - my_tp

    def group(step):
        first = lax.rem(my_z + step, outer) * INNER * rows
        return pl.ds(pl.multiple_of(first, rows), INNER * rows)

    def token_rows(step, x):
        first = (lax.rem(my_z + step, outer) * INNER + x) * rows
        return pl.ds(pl.multiple_of(first, rows), rows)

    vector_core = copies.start(vectors, core_vector, sibling)
    order = list(range(1, outer)) + [0]
    over_core = {}
    for step in order:
        here = group(step)
        over_core[step] = copies.start(
            partial.at[other_core, here], from_core.at[here], sibling
        )
    over_y = []
    for other in range(1, dp):
        target = lax.rem(my_dp + other, dp)
        over_y.append(copies.start(grads.at[target], from_y.at[other - 1], {"dp": target}))

    over_x = {}
    for step in order:
        over_core[step].wait_recv()
        there = token_rows(step, INNER - 1 - my_x)
        to_x[step] = (
            partial[my_tp, there, :].astype(f32) + from_core[there, :].astype(f32)
        ).astype(bf16)
        over_x[step] = copies.start(to_x.at[step], from_x.at[step], partner)

    vector_core.wait_recv()
    passed_vector[0] = vectors[...] + core_vector[...]
    vector_x = copies.start(passed_vector.at[0], x_vector, partner)

    def own_sum(step):
        here = token_rows(step, my_x)
        local = partial[my_tp, here, :].astype(f32) + from_core[here, :].astype(f32)
        return local + from_x[step].astype(f32)

    over_z = {}
    for step in range(1, outer):
        over_x[step].wait_recv()
        to_z[step - 1] = own_sum(step).astype(bf16)
        target = lax.rem(my_z + step, outer) * INNER + my_x
        over_z[step] = copies.start(to_z.at[step - 1], from_z.at[step - 1], {"ctx": target})

    vector_x.wait_recv()
    passed_vector[1] = passed_vector[0] + x_vector[...]
    z_vectors[my_z] = passed_vector[1]
    vector_z = []
    for step in range(1, outer):
        target = lax.rem(my_z + step, outer) * INNER + my_x
        vector_z.append(
            copies.start(passed_vector.at[1], z_vectors.at[my_z], {"ctx": target})
        )

    for copy in over_y:
        copy.wait_recv()
    over_ctx = []
    for step in list(range(1, ctx)) + [0]:
        target = lax.rem(my_ctx + step, ctx)
        total = grads[my_dp, target].astype(f32)
        for other in range(1, dp):
            total = total + from_y[other - 1, target].astype(f32)
        summed[step] = total.astype(bf16)
        if step > 0:
            over_ctx.append(
                copies.start(summed.at[step], own_grads.at[my_ctx], {"ctx": target})
            )
    own = pltpu.make_async_copy(summed.at[0], own_grads.at[my_ctx], local_sem)
    own.start()

    for copy in vector_z:
        copy.wait_recv()
    total = z_vectors[0]
    for place in range(1, outer):
        total = total + z_vectors[place]
    passed_vector[2] = total
    y_vectors[my_dp] = total
    vector_y = []
    for other in range(1, dp):
        target = {"dp": lax.rem(my_dp + other, dp)}
        vector_y.append(copies.start(passed_vector.at[2], y_vectors.at[my_dp], target))

    over_x[0].wait_recv()
    result = own_sum(0)
    for step in range(1, outer):
        over_z[step].wait_recv()
        result = result + from_z[step - 1].astype(f32)
    sums[...] = result
    for copy in vector_y:
        copy.wait_recv()
    total = y_vectors[0]
    for place in range(1, dp):
        total = total + y_vectors[place]
    totals[...] = total
    for copy in over_ctx:
        copy.wait_recv()
    copies.finish()
    own.wait()


def reduce_all(partial, grads, vectors, dp, ctx, tp):
    outer = ctx // INNER
    rows, width = partial.shape[1] // ctx, partial.shape[2]
    block = grads.shape[2:]
    bf16 = jnp.bfloat16
    count = outer + (dp - 1) + outer + (outer - 1) + (ctx - 1)
    count += 2 + (outer - 1) + (dp - 1)
    vmem = pl.BlockSpec(memory_space=pltpu.VMEM)
    return pl.pallas_call(
        functools.partial(reduce_kernel, ctx, dp, tp),
        out_shape=(
            jax.ShapeDtypeStruct((rows, width), jnp.float32),
            jax.ShapeDtypeStruct((ctx,) + block, bf16),
            jax.ShapeDtypeStruct(vectors.shape, jnp.float32),
        ),
        in_specs=[vmem] * 3,
        out_specs=(vmem, pl.BlockSpec(memory_space=pl.ANY), vmem),
        scratch_shapes=[
            pltpu.VMEM(partial.shape[1:], bf16),
            pltpu.VMEM((outer, rows, width), bf16),
            pltpu.VMEM((outer, rows, width), bf16),
            pltpu.VMEM((outer - 1, rows, width), bf16),
            pltpu.VMEM((outer - 1, rows, width), bf16),
            pltpu.VMEM((dp - 1, ctx) + block, bf16),
            pltpu.VMEM((ctx,) + block, bf16),
            pltpu.VMEM(vectors.shape, jnp.float32),
            pltpu.VMEM(vectors.shape, jnp.float32),
            pltpu.VMEM((3,) + vectors.shape, jnp.float32),
            pltpu.VMEM((outer,) + vectors.shape, jnp.float32),
            pltpu.VMEM((dp,) + vectors.shape, jnp.float32),
            pltpu.SemaphoreType.DMA((count,)),
            pltpu.SemaphoreType.DMA((count,)),
            pltpu.SemaphoreType.DMA,
        ],
        compiler_params=pltpu.CompilerParams(
            collective_id=1, has_side_effects=True, vmem_limit_bytes=48 * 2**20
        ),
    )(partial, grads, vectors)


def on_device(
    inputs,
    segments,
    gain_one,
    bias_one,
    gain_two,
    bias_two,
    w_qkv,
    b_qkv,
    w_out,
    out_bias,
    w_up,
    b_up,
    w_down,
    cotangent,
):
    f32, bf16 = jnp.float32, jnp.bfloat16
    dp, ctx, tp = lax.axis_size("dp"), lax.axis_size("ctx"), lax.axis_size("tp")
    my_ctx, my_tp = lax.axis_index("ctx"), lax.axis_index("tp")
    local_rows, width = inputs.shape[1:]
    length = local_rows * ctx
    share = width // tp
    owned = w_qkv.shape[0]
    heads = w_qkv.shape[2] // HD
    slots = -(-heads // ctx)
    head_width = slots * HD
    units = w_up.shape[1] // ctx
    pad_heads = slots * ctx * HD - heads * HD

    qkv_blocks = jnp.pad(w_qkv, ((0, 0), (0, 0), (0, pad_heads)))
    qkv_blocks = qkv_blocks.reshape(owned, 3, ctx, head_width).transpose(2, 0, 1, 3)
    out_blocks = jnp.pad(w_out, ((0, 0), (0, pad_heads))).reshape(owned, ctx, head_width)
    blocks = jnp.concatenate(
        [
            w_down.reshape(owned, ctx, units).transpose(1, 0, 2),
            out_blocks.transpose(1, 0, 2),
            w_up.reshape(owned, ctx, units).transpose(1, 0, 2),
            qkv_blocks.reshape(ctx, owned, 3 * head_width),
        ],
        axis=-1,
    )
    block_width = blocks.shape[-1]
    pad_rows, pad_width = -owned % 16, -block_width % 128
    blocks = jnp.pad(blocks, ((0, 0), (0, pad_rows), (0, pad_width)))
    seg_columns = jnp.broadcast_to(segments[0].astype(bf16)[:, None], (local_rows, 128))
    packed = jnp.concatenate([inputs[0], cotangent[0], seg_columns], axis=-1)
    row, columns = gather_all(packed, blocks, dp, ctx, tp)
    columns = columns[:, :, :owned, :block_width].reshape(width, -1)
    qkv_bias = jnp.pad(b_qkv, ((0, 0), (0, pad_heads))).reshape(3, ctx, head_width)
    qkv_bias = lax.dynamic_index_in_dim(qkv_bias, my_ctx, 1, keepdims=False).reshape(-1)
    up_bias = lax.dynamic_slice_in_dim(b_up, my_ctx * units, units, 0)

    cosine_table, sine_table = angle_tables(0, length)
    rest = jnp.zeros((length, HD - ROT), f32)
    cosines = jnp.concatenate([cosine_table, cosine_table, rest + 1.0], axis=-1)
    sines = jnp.concatenate([sine_table, sine_table, rest], axis=-1)
    norms = jnp.stack([gain_one, bias_one, gain_two, bias_two])
    partial, grads, norm_grads, grad_b_up, grad_b_qkv = compute_all(
        row,
        columns,
        jnp.concatenate([cosines, cosines], axis=-1),
        jnp.concatenate([sines, sines], axis=-1),
        norms,
        up_bias[None],
        qkv_bias[None],
        width,
        units,
        share,
    )

    grads = grads.reshape(dp, ctx, owned, -1)
    grads = jnp.pad(grads, ((0, 0), (0, 0), (0, pad_rows), (0, pad_width)))

    grad_bias = jnp.sum(cotangent[0].astype(f32), axis=0) * (my_tp == 0).astype(f32)
    place = (jnp.arange(tp)[:, None] == my_tp) & (jnp.arange(ctx)[None, :] == my_ctx)
    local = jnp.concatenate([grad_b_qkv[0], grad_b_up[0]])
    spread = jnp.where(place[:, :, None], local, 0.0)
    vectors = jnp.concatenate(
        [
            norm_grads.reshape(-1),
            grad_bias,
            spread.reshape(-1),
        ]
    )
    vector_size = vectors.shape[0]
    vectors = jnp.pad(vectors, (0, -vector_size % 1024)).reshape(-1, 128)
    sums, own, total = reduce_all(partial, grads, vectors, dp, ctx, tp)
    branch_share, input_share = sums[:, :share], sums[:, share:]
    own = own[:, :owned, :block_width].astype(f32)
    own_down = own[:, :, :units].transpose(1, 0, 2).reshape(owned, -1)
    own_out = own[:, :, units : units + head_width].transpose(1, 0, 2)
    own_out = own_out.reshape(owned, -1)[:, : heads * HD]
    first = units + head_width
    own_up = own[:, :, first : first + units].transpose(1, 0, 2).reshape(owned, -1)
    own_qkv = own[:, :, first + units :].reshape(ctx, owned, 3, head_width)
    own_qkv = own_qkv.transpose(1, 2, 0, 3).reshape(owned, 3, ctx * head_width)
    own_qkv = own_qkv[:, :, : heads * HD]
    total = total.reshape(-1)[:vector_size]
    spread = total[5 * width :].reshape(tp, ctx, -1)
    spread = lax.dynamic_index_in_dim(spread, my_tp, 0, keepdims=False)
    sum_b_qkv = spread[:, : 3 * head_width].reshape(ctx, 3, head_width).transpose(1, 0, 2)
    sum_b_qkv = sum_b_qkv.reshape(3, -1)[:, : heads * HD]
    sum_b_up = spread[:, 3 * head_width :].reshape(-1)

    start = my_tp * share
    token_share = lax.dynamic_slice_in_dim(inputs[0], start, share, 1).astype(f32)
    bias_share = lax.dynamic_slice_in_dim(out_bias, start, share, 0)
    cotangent_share = lax.dynamic_slice_in_dim(cotangent[0], start, share, 1).astype(f32)
    output = token_share + branch_share + bias_share
    grad_inputs = cotangent_share + input_share
    return (
        output[None],
        grad_inputs[None],
        total[:width],
        total[width : 2 * width],
        total[2 * width : 3 * width],
        total[3 * width : 4 * width],
        own_qkv,
        sum_b_qkv,
        own_out,
        total[4 * width : 5 * width],
        own_up,
        sum_b_up,
        own_down,
    )


def solution(mesh):
    return jax.shard_map(
        on_device,
        mesh=mesh,
        in_specs=(
            P("dp", "ctx", None),
            P("dp", "ctx"),
            P(),
            P(),
            P(),
            P(),
            P(("dp", "ctx"), None, "tp"),
            P(None, "tp"),
            P(("dp", "ctx"), "tp"),
            P(),
            P(("dp", "ctx"), "tp"),
            P("tp"),
            P(("dp", "ctx"), "tp"),
            P("dp", "ctx", None),
        ),
        out_specs=(
            P("dp", "ctx", "tp"),
            P("dp", "ctx", "tp"),
            P(),
            P(),
            P(),
            P(),
            P(("dp", "ctx"), None, "tp"),
            P(None, "tp"),
            P(("dp", "ctx"), "tp"),
            P(),
            P(("dp", "ctx"), "tp"),
            P("tp"),
            P(("dp", "ctx"), "tp"),
        ),
        check_vma=False,
    )
```

```python
import functools
import math

import jax
import jax.numpy as jnp
from jax import lax
from jax.experimental import pallas as pl
from jax.experimental.pallas import tpu as pltpu
import numpy as np
from jax.sharding import PartitionSpec as P

HD = 64
ROT = 16

NORM_EPSILON = 1e-05
NEG_LARGE = -1e30
LAST = (((1,), (1,)), ((), ()))
ROWS = (((0,), (0,)), ((), ()))


def dot_f32(a, b, dims=(((1,), (0,)), ((), ()))):
    return lax.dot_general(a, b, dims, preferred_element_type=jnp.float32)


def angle_tables(length):
    frequency = np.float32(10000.0) ** (-(np.arange(ROT // 2, dtype=np.float32) * 2.0 / ROT))
    angles = np.arange(length, dtype=np.float32)[:, None] * frequency.astype(np.float32)
    rest = np.zeros((length, HD - ROT))
    angles = angles.astype(np.float64)
    cosines = np.concatenate([np.cos(angles), np.cos(angles), rest + 1.0], axis=-1)
    sines = np.concatenate([np.sin(angles), np.sin(angles), rest], axis=-1)
    return tuple(np.concatenate([t, t], axis=-1).astype(np.float32) for t in (cosines, sines))


def swap_matrix(size):
    source = lax.broadcasted_iota(jnp.int32, (size, size), 0)
    target = lax.broadcasted_iota(jnp.int32, (size, size), 1)
    dim = lax.rem(target, HD)
    half_rot = ROT // 2
    minus = (dim < half_rot) & (source == target + half_rot)
    plus = (dim >= half_rot) & (dim < ROT) & (source == target - half_rot)
    return jnp.where(plus, 1.0, 0.0) - jnp.where(minus, 1.0, 0.0)


def swapped(values, matrix):
    return lax.dot_general(
        values,
        matrix,
        (((1,), (0,)), ((), ())),
        preferred_element_type=jnp.float32,
        precision=lax.Precision.HIGHEST,
    )


class Tree:
    def __init__(self, copies, place, partial, from_core, to_x, from_x, to_z, from_z):
        self.copies, self.place, self.partial, self.from_core = copies, place, partial, from_core
        self.to_x, self.from_x, self.to_z, self.from_z = to_x, from_x, to_z, from_z
        self.over_core, self.over_x, self.over_z = {}, {}, {}

    def send_core(self, step):
        here = self.place.group(step)
        self.over_core[step] = self.copies.start(
            self.partial.at[1 - self.place.tp, here], self.from_core.at[here], self.place.sibling
        )

    def local_sum(self, step, x):
        here = self.place.token_rows(step, x)
        mine = self.partial[self.place.tp, here, :].astype(jnp.float32)
        return mine + self.from_core[here, :].astype(jnp.float32)

    def send_x(self, step):
        self.over_core[step].wait_recv()
        self.to_x[step] = self.local_sum(step, INNER - 1 - self.place.x).astype(jnp.bfloat16)
        self.over_x[step] = self.copies.start(
            self.to_x.at[step], self.from_x.at[step], self.place.partner
        )

    def x_sum(self, step):
        self.over_x[step].wait_recv()
        local = self.local_sum(step, self.place.x)
        return local + self.from_x[step].astype(jnp.float32)

    def send_z(self, step):
        self.to_z[step - 1] = self.x_sum(step).astype(jnp.bfloat16)
        self.over_z[step] = self.copies.start(
            self.to_z.at[step - 1], self.from_z.at[step - 1], self.place.along(step)
        )

    def result(self):
        total = self.x_sum(0)
        for step in range(1, self.place.outer):
            self.over_z[step].wait_recv()
            total = total + self.from_z[step - 1].astype(jnp.float32)
        return total


class Place:
    def __init__(self, ctx, dp, tp, rows):
        self.outer, self.rows = ctx // INNER, rows
        self.ctx, self.dp, self.tp = (lax.axis_index(name) for name in ("ctx", "dp", "tp"))
        self.z, self.x = self.ctx // INNER, lax.rem(self.ctx, INNER)
        self.partner = {"ctx": self.z * INNER + (INNER - 1 - self.x)}
        self.sibling = {"tp": tp - 1 - self.tp}

    def along(self, step):
        return {"ctx": lax.rem(self.z + step, self.outer) * INNER + self.x}

    def group(self, step):
        first = lax.rem(self.z + step, self.outer) * INNER * self.rows
        return pl.ds(pl.multiple_of(first, INNER * self.rows), INNER * self.rows)

    def token_rows(self, step, x):
        first = (lax.rem(self.z + step, self.outer) * INNER + x) * self.rows
        return pl.ds(pl.multiple_of(first, self.rows), self.rows)


class Exchange:
    def __init__(self, copies, place, ctx, dp, grads, from_y, summed, own_grads, local_sem):
        self.copies, self.place, self.ctx, self.dp = copies, place, ctx, dp
        self.grads, self.from_y, self.summed = grads, from_y, summed
        self.own_grads, self.local_sem = own_grads, local_sem

    def send_y(self):
        self.over_y = []
        for other in range(1, self.dp):
            target = lax.rem(self.place.dp + other, self.dp)
            self.over_y.append(
                self.copies.start(
                    self.grads.at[target], self.from_y.at[other - 1], {"dp": target}
                )
            )

    def send_ctx(self):
        for copy in self.over_y:
            copy.wait_recv()
        self.over_ctx = []
        for step in list(range(1, self.ctx)) + [0]:
            target = lax.rem(self.place.ctx + step, self.ctx)
            total = self.grads[self.place.dp, target].astype(jnp.float32)
            for other in range(1, self.dp):
                total = total + self.from_y[other - 1, target].astype(jnp.float32)
            self.summed[step] = total.astype(jnp.bfloat16)
            if step > 0:
                self.over_ctx.append(
                    self.copies.start(
                        self.summed.at[step], self.own_grads.at[self.place.ctx], {"ctx": target}
                    )
                )
        self.own = pltpu.make_async_copy(
            self.summed.at[0], self.own_grads.at[self.place.ctx], self.local_sem
        )
        self.own.start()

    def finish(self):
        for copy in self.over_ctx:
            copy.wait_recv()
        self.own.wait()


def compute_kernel(
    width,
    units,
    share,
    ctx,
    dp,
    tp,
    owned,
    row,
    columns,
    cosines,
    sines,
    norms,
    up_bias,
    qkv_bias,
    sums,
    early_own,
    late_own,
    totals,
    norm_grads,
    local_vector,
    averages,
    inverses,
    norm_one,
    norm_two,
    queries,
    keys,
    values,
    mixed,
    grad_attended,
    grad_pre,
    grad_query,
    grad_key,
    grad_value,
    grad_projected,
    hot,
    out_partial,
    out_core,
    out_to_x,
    out_from_x,
    out_to_z,
    out_from_z,
    in_partial,
    in_core,
    in_to_x,
    in_from_x,
    in_to_z,
    in_from_z,
    early_grads,
    early_y,
    early_sum,
    late_grads,
    late_y,
    late_sum,
    vectors,
    core_vector,
    x_vector,
    passed_vector,
    z_vectors,
    y_vectors,
    send_sems,
    recv_sems,
    local_sems,
):
    f32, bf16 = jnp.float32, jnp.bfloat16
    length = row.shape[0]
    rows = length // ctx
    place = Place(ctx, dp, tp, rows)
    greet(ctx, dp, tp, place.ctx, place.dp, place.tp)
    copies = Copies(send_sems, recv_sems)
    out_tree = Tree(
        copies, place, out_partial, out_core, out_to_x, out_from_x, out_to_z, out_from_z
    )
    in_tree = Tree(copies, place, in_partial, in_core, in_to_x, in_from_x, in_to_z, in_from_z)
    early = Exchange(
        copies, place, ctx, dp, early_grads, early_y, early_sum, early_own, local_sems.at[0]
    )
    late = Exchange(
        copies, place, ctx, dp, late_grads, late_y, late_sum, late_own, local_sems.at[1]
    )
    order = list(range(1, place.outer)) + [0]
    tile = INNER * rows
    tiles = length // tile
    both = units + HD
    scale = 1.0 / math.sqrt(HD)
    matrix = swap_matrix(2 * HD)
    norm_grads[...] = jnp.zeros_like(norm_grads)
    local_vector[...] = jnp.zeros_like(local_vector)
    grad_key[...] = jnp.zeros_like(grad_key)
    grad_value[...] = jnp.zeros_like(grad_value)

    def first_pass(step, carry):
        here = pl.ds(pl.multiple_of(step * tile, tile), tile)
        tokens = row[here, :width].astype(f32)
        average = jnp.mean(tokens, axis=-1, keepdims=True)
        centered = tokens - average
        variance = jnp.mean(centered * centered, axis=-1, keepdims=True)
        inverse = lax.rsqrt(variance + NORM_EPSILON)
        xhat = centered * inverse
        averages[here, :] = average
        inverses[here, :] = inverse
        one = (xhat * norms[0:1, :] + norms[1:2, :]).astype(bf16)
        two = (xhat * norms[2:3, :] + norms[3:4, :]).astype(bf16)
        norm_one[here, :] = one
        norm_two[here, :] = two
        projected = dot_f32(one, columns[:, both + units :]) + qkv_bias[...]
        turning = projected[:, : 2 * HD]
        turned = turning * cosines[here, :] + swapped(turning, matrix) * sines[here, :]
        queries[here, :] = (turned[:, :HD].astype(bf16).astype(f32) * scale).astype(bf16)
        keys[here, :] = turned[:, HD:].astype(bf16)
        values[here, :] = projected[:, 2 * HD :].astype(bf16)
        lane = lax.broadcasted_iota(jnp.int32, (tile, 128), 1).astype(f32)
        segment = row[here, 2 * width :].astype(f32)
        hot[here, :] = jnp.where(segment == lane, 1.0, 0.0).astype(bf16)
        pre = dot_f32(two, columns[:, both : both + units]) + up_bias[...]
        cumulative = 0.5 * (1.0 + lax.erf(pre * math.sqrt(0.5)))
        density = jnp.exp(pre * pre * -0.5) * (1.0 / math.sqrt(2.0 * math.pi))
        mixed[here, :units] = (pre * cumulative).astype(bf16)
        grad_mixed = dot_f32(row[here, width : 2 * width], columns[:, :both])
        slope = (grad_mixed[:, :units] * (cumulative + pre * density)).astype(bf16)
        grad_pre[here, :] = slope
        local_vector[:, 3 * HD : 3 * HD + units] += jnp.sum(slope.astype(f32), axis=0, keepdims=True)
        grad_attended[here, :] = grad_mixed[:, units:].astype(bf16)
        return carry

    lax.fori_loop(0, tiles, first_pass, 0)

    def weight_grads(store, first, left, left_first, right):
        block = ctx * owned
        for half in range(dp):
            rows_here = left[:, left_first + half * block : left_first + (half + 1) * block]
            grad = dot_f32(rows_here, right, ROWS)
            for owner in range(ctx):
                store[half, owner, :owned, first : first + right.shape[1]] = grad[
                    owner * owned : (owner + 1) * owned
                ].astype(bf16)

    weight_grads(early_grads, 0, row, width, mixed[:, :units])
    weight_grads(early_grads, units, norm_two, 0, grad_pre[...])
    early.send_y()

    for step in range(tiles):
        here = pl.ds(step * tile, tile)
        seen = (step + 1) * tile
        query, key, value = queries[here, :], keys[:seen, :], values[:seen, :]
        scores = dot_f32(query, key, LAST)
        same = dot_f32(hot[here, :], hot[:seen, :], LAST) > 0.5
        at_query = lax.broadcasted_iota(jnp.int32, (tile, seen), 0) + step * tile
        at_key = lax.broadcasted_iota(jnp.int32, (tile, seen), 1)
        scores = jnp.where(same & (at_key <= at_query), scores, NEG_LARGE)
        exponent = jnp.exp(scores - jnp.max(scores, axis=-1, keepdims=True))
        softmax = exponent / jnp.sum(exponent, axis=-1, keepdims=True)
        softmax_low = softmax.astype(bf16)
        attended = dot_f32(softmax_low, value)
        mixed[here, units:] = attended.astype(bf16)
        grad_rows = grad_attended[here, :]
        grad_dots = jnp.sum(grad_rows.astype(f32) * attended, axis=-1, keepdims=True)
        grad_probs = dot_f32(grad_rows, value, LAST)
        grad_scores = (softmax * (grad_probs - grad_dots)).astype(bf16)
        grad_query[here, :] = dot_f32(grad_scores, key) * scale
        grad_key[:, :seen] += dot_f32(query, grad_scores, ROWS)
        grad_value[:, :seen] += dot_f32(grad_rows, softmax_low, ROWS)
        if step == min(1, tiles - 1):
            early.send_ctx()

    for step in order:
        here = place.group(step)
        branch = dot_f32(mixed[here, :], columns[:, :both], LAST).astype(bf16)
        for part in range(tp):
            out_partial[part, here, :] = branch[:, part * share : (part + 1) * share]
        out_tree.send_core(step)

    for step in range(tiles):
        here = pl.ds(step * tile, tile)
        key_rows = grad_key[:, step * tile : (step + 1) * tile].T
        value_rows = grad_value[:, step * tile : (step + 1) * tile].T
        turning = jnp.concatenate([grad_query[here, :], key_rows], axis=-1)
        turned = turning * cosines[here, :] - swapped(turning, matrix) * sines[here, :]
        pulled = jnp.concatenate([turned, value_rows], axis=-1).astype(bf16)
        grad_projected[here, :] = pulled
        local_vector[:, : 3 * HD] += jnp.sum(pulled.astype(f32), axis=0, keepdims=True)

    weight_grads(late_grads, 0, row, width, mixed[:, units:])
    weight_grads(late_grads, HD, norm_one, 0, grad_projected[...])
    late.send_y()

    for step in order:
        out_tree.send_x(step)
        here = place.group(step)
        xhat = (row[here, :width].astype(f32) - averages[here, :]) * inverses[here, :]
        grad_one = dot_f32(grad_projected[here, :], columns[:, both + units :], LAST)
        grad_two = dot_f32(grad_pre[here, :], columns[:, both : both + units], LAST)
        norm_grads[0:1, :] += jnp.sum(grad_one * xhat, axis=0, keepdims=True)
        norm_grads[1:2, :] += jnp.sum(grad_one, axis=0, keepdims=True)
        norm_grads[2:3, :] += jnp.sum(grad_two * xhat, axis=0, keepdims=True)
        norm_grads[3:4, :] += jnp.sum(grad_two, axis=0, keepdims=True)
        pulled = grad_one * norms[0:1, :] + grad_two * norms[2:3, :]
        term = inverses[here, :] * (
            pulled
            - jnp.mean(pulled, axis=-1, keepdims=True)
            - xhat * jnp.mean(pulled * xhat, axis=-1, keepdims=True)
        )
        term = term.astype(bf16)
        for part in range(tp):
            in_partial[part, here, :] = term[:, part * share : (part + 1) * share]
        in_tree.send_core(step)

    for step in order:
        in_tree.send_x(step)
        if step > 0:
            out_tree.send_z(step)

    own_rows = row[place.token_rows(0, place.x), width : 2 * width].astype(f32)
    out_bias_grad = jnp.sum(own_rows, axis=0, keepdims=True)
    out_bias_grad = jnp.where(place.tp == 0, out_bias_grad, 0.0)
    vectors[...] = jnp.zeros_like(vectors)
    lines = width // 128
    for line in range(lines):
        lanes = slice(line * 128, (line + 1) * 128)
        for item in range(4):
            vectors[item * lines + line : item * lines + line + 1, :] = norm_grads[
                item : item + 1, lanes
            ]
        vectors[4 * lines + line : 4 * lines + line + 1, :] = out_bias_grad[:, lanes]
    slot_lines = local_vector.shape[1] // 128
    first_line = 5 * lines + (place.tp * ctx + place.ctx) * slot_lines
    for line in range(slot_lines):
        vectors[pl.ds(first_line + line, 1), :] = local_vector[:, line * 128 : (line + 1) * 128]
    vector_core = copies.start(vectors, core_vector, place.sibling)

    late.send_ctx()
    vector_core.wait_recv()
    passed_vector[0] = vectors[...] + core_vector[...]
    vector_x = copies.start(passed_vector.at[0], x_vector, place.partner)
    for step in range(1, place.outer):
        in_tree.send_z(step)
    vector_x.wait_recv()
    passed_vector[1] = passed_vector[0] + x_vector[...]
    z_vectors[place.z] = passed_vector[1]
    vector_z = [
        copies.start(passed_vector.at[1], z_vectors.at[place.z], place.along(step))
        for step in range(1, place.outer)
    ]
    sums[:, :share] = out_tree.result()
    for copy in vector_z:
        copy.wait_recv()
    total = z_vectors[0]
    for other in range(1, place.outer):
        total = total + z_vectors[other]
    passed_vector[2] = total
    y_vectors[place.dp] = total
    vector_y = [
        copies.start(
            passed_vector.at[2], y_vectors.at[place.dp], {"dp": lax.rem(place.dp + other, dp)}
        )
        for other in range(1, dp)
    ]
    sums[:, share:] = in_tree.result()
    for copy in vector_y:
        copy.wait_recv()
    total = y_vectors[0]
    for other in range(1, dp):
        total = total + y_vectors[other]
    totals[...] = total
    early.finish()
    late.finish()
    copies.finish()


def compute_all(
    row, columns, cosines, sines, norms, up_bias, qkv_bias, width, units, share, ctx, dp, tp, owned
):
    f32, bf16 = jnp.float32, jnp.bfloat16
    length = row.shape[0]
    outer, rows = ctx // INNER, length // ctx
    padded = owned + -owned % 16
    early_width = 2 * units + -2 * units % 128
    late_width = 4 * HD
    slot = 3 * HD + units
    slot += -slot % 128
    lines = 5 * width // 128 + tp * ctx * slot // 128
    lines += -lines % 8
    vmem = pl.BlockSpec(memory_space=pltpu.VMEM)
    anywhere = pl.BlockSpec(memory_space=pl.ANY)
    tree = [
        pltpu.VMEM((tp, length, share), bf16),
        pltpu.VMEM((length, share), bf16),
        pltpu.VMEM((outer, rows, share), bf16),
        pltpu.VMEM((outer, rows, share), bf16),
        pltpu.VMEM((outer - 1, rows, share), bf16),
        pltpu.VMEM((outer - 1, rows, share), bf16),
    ]

    def exchange(block_width):
        return [
            pltpu.VMEM((dp, ctx, padded, block_width), bf16),
            pltpu.VMEM((dp - 1, ctx, padded, block_width), bf16),
            pltpu.VMEM((ctx, padded, block_width), bf16),
        ]

    count = 2 * (3 * outer - 1) + 2 * (dp - 1 + ctx - 1) + 2 + (outer - 1) + (dp - 1)
    vector = (lines, 128)
    return pl.pallas_call(
        functools.partial(compute_kernel, width, units, share, ctx, dp, tp, owned),
        out_shape=(
            jax.ShapeDtypeStruct((rows, 2 * share), f32),
            jax.ShapeDtypeStruct((ctx, padded, early_width), bf16),
            jax.ShapeDtypeStruct((ctx, padded, late_width), bf16),
            jax.ShapeDtypeStruct(vector, f32),
        ),
        in_specs=[vmem] * 7,
        out_specs=(vmem, anywhere, anywhere, vmem),
        scratch_shapes=[
            pltpu.VMEM((4, width), f32),
            pltpu.VMEM((1, slot), f32),
            pltpu.VMEM((length, 1), f32),
            pltpu.VMEM((length, 1), f32),
            pltpu.VMEM((length, width), bf16),
            pltpu.VMEM((length, width), bf16),
            pltpu.VMEM((length, HD), bf16),
            pltpu.VMEM((length, HD), bf16),
            pltpu.VMEM((length, HD), bf16),
            pltpu.VMEM((length, units + HD), bf16),
            pltpu.VMEM((length, HD), bf16),
            pltpu.VMEM((length, units), bf16),
            pltpu.VMEM((length, HD), f32),
            pltpu.VMEM((HD, length), f32),
            pltpu.VMEM((HD, length), f32),
            pltpu.VMEM((length, 3 * HD), bf16),
            pltpu.VMEM((length, 128), bf16),
        ]
        + tree
        + tree
        + exchange(early_width)
        + exchange(late_width)
        + [
            pltpu.VMEM(vector, f32),
            pltpu.VMEM(vector, f32),
            pltpu.VMEM(vector, f32),
            pltpu.VMEM((3,) + vector, f32),
            pltpu.VMEM((outer,) + vector, f32),
            pltpu.VMEM((dp,) + vector, f32),
            pltpu.SemaphoreType.DMA((count,)),
            pltpu.SemaphoreType.DMA((count,)),
            pltpu.SemaphoreType.DMA((2,)),
        ],
        compiler_params=pltpu.CompilerParams(
            collective_id=1, has_side_effects=True, vmem_limit_bytes=60 * 2**20
        ),
    )(row, columns, cosines, sines, norms, up_bias, qkv_bias)


MESH = pl.DeviceIdType.MESH
INNER = 2


def greet(ctx, dp, tp, my_ctx, my_dp, my_tp):
    barrier = pltpu.get_barrier_semaphore()
    for step in range(1, ctx):
        peer = {"ctx": lax.rem(my_ctx + step, ctx)}
        pl.semaphore_signal(barrier, inc=1, device_id=peer, device_id_type=MESH)
    for step in range(1, dp):
        peer = {"dp": lax.rem(my_dp + step, dp)}
        pl.semaphore_signal(barrier, inc=1, device_id=peer, device_id_type=MESH)
    for step in range(1, tp):
        peer = {"tp": lax.rem(my_tp + step, tp)}
        pl.semaphore_signal(barrier, inc=1, device_id=peer, device_id_type=MESH)
    pl.semaphore_wait(barrier, ctx + dp + tp - 3)


class Copies:
    def __init__(self, send_sems, recv_sems):
        self.send_sems, self.recv_sems, self.items = send_sems, recv_sems, []

    def start(self, src, dst, peer):
        place = len(self.items)
        copy = pltpu.make_async_remote_copy(
            src_ref=src,
            dst_ref=dst,
            send_sem=self.send_sems.at[place],
            recv_sem=self.recv_sems.at[place],
            device_id=peer,
            device_id_type=MESH,
        )
        copy.start()
        self.items.append(copy)
        return copy

    def finish(self):
        for copy in self.items:
            copy.wait_send()


def gather_kernel(
    ctx, dp, tp, packed, blocks, row, columns, send_sems, recv_sems, local_sems
):
    my_ctx, my_dp, my_tp = lax.axis_index("ctx"), lax.axis_index("dp"), lax.axis_index("tp")
    outer = ctx // INNER
    my_z, my_x = my_ctx // INNER, lax.rem(my_ctx, INNER)
    rows = packed.shape[0]
    half = rows // tp

    def piece(owner, core):
        return row.at[pl.ds(pl.multiple_of(owner * rows + core * half, half), half)]

    own_row = pltpu.make_async_copy(
        packed, row.at[pl.ds(pl.multiple_of(my_ctx * rows, rows), rows)], local_sems.at[0]
    )
    own_block = pltpu.make_async_copy(
        blocks.at[my_ctx], columns.at[my_dp, my_ctx], local_sems.at[1]
    )
    own_row.start()
    own_block.start()
    greet(ctx, dp, tp, my_ctx, my_dp, my_tp)
    copies = Copies(send_sems, recv_sems)
    mine = packed.at[pl.ds(pl.multiple_of(my_tp * half, half), half)]
    partner = {"ctx": my_z * INNER + (INNER - 1 - my_x)}
    sibling = {"tp": tp - 1 - my_tp}
    along = []
    for step in range(1, outer):
        target = lax.rem(my_z + step, outer) * INNER + my_x
        along.append(copies.start(mine, piece(my_ctx, my_tp), {"ctx": target}))
    across = [copies.start(mine, piece(my_ctx, my_tp), partner)]
    exchanged = []
    for step in range(1, ctx):
        target = lax.rem(my_ctx + step, ctx)
        exchanged.append(
            copies.start(blocks.at[target], columns.at[my_dp, my_ctx], {"ctx": target})
        )
    to_sibling = []
    for step in range(1, outer):
        source = lax.rem(my_z + outer - step, outer) * INNER + my_x
        along[step - 1].wait_recv()
        across.append(copies.start(piece(source, my_tp), piece(source, my_tp), partner))
        to_sibling.append(copies.start(piece(source, my_tp), piece(source, my_tp), sibling))
    over_dp = []
    for other in range(1, dp):
        target = {"dp": lax.rem(my_dp + other, dp)}
        over_dp.append(
            copies.start(blocks.at[my_ctx], columns.at[my_dp, my_ctx], target)
        )
    for step in range(1, ctx):
        source = lax.rem(my_ctx + ctx - step, ctx)
        exchanged[step - 1].wait_recv()
        for other in range(1, dp):
            target = {"dp": lax.rem(my_dp + other, dp)}
            over_dp.append(
                copies.start(columns.at[my_dp, source], columns.at[my_dp, source], target)
            )
    for step in range(outer):
        source = lax.rem(my_z + outer - step, outer) * INNER + (INNER - 1 - my_x)
        across[step].wait_recv()
        to_sibling.append(copies.start(piece(source, my_tp), piece(source, my_tp), sibling))
    for copy in over_dp + to_sibling:
        copy.wait_recv()
    copies.finish()
    own_row.wait()
    own_block.wait()


def gather_all(packed, blocks, dp, ctx, tp):
    outer = ctx // INNER
    count = (outer - 1) + outer + (ctx - 1) + (2 * outer - 1) + ctx * (dp - 1)
    return pl.pallas_call(
        functools.partial(gather_kernel, ctx, dp, tp),
        out_shape=(
            jax.ShapeDtypeStruct((ctx * packed.shape[0], packed.shape[1]), packed.dtype),
            jax.ShapeDtypeStruct((dp,) + blocks.shape, blocks.dtype),
        ),
        in_specs=[pl.BlockSpec(memory_space=pl.ANY)] * 2,
        out_specs=(pl.BlockSpec(memory_space=pl.ANY),) * 2,
        scratch_shapes=[
            pltpu.SemaphoreType.DMA((count,)),
            pltpu.SemaphoreType.DMA((count,)),
            pltpu.SemaphoreType.DMA((2,)),
        ],
        compiler_params=pltpu.CompilerParams(collective_id=0, has_side_effects=True),
    )(packed, blocks)


def on_device(
    inputs,
    segments,
    gain_one,
    bias_one,
    gain_two,
    bias_two,
    w_qkv,
    b_qkv,
    w_out,
    out_bias,
    w_up,
    b_up,
    w_down,
    cotangent,
):
    f32, bf16 = jnp.float32, jnp.bfloat16
    dp, ctx, tp = lax.axis_size("dp"), lax.axis_size("ctx"), lax.axis_size("tp")
    my_ctx, my_tp = lax.axis_index("ctx"), lax.axis_index("tp")
    local_rows, width = inputs.shape[1:]
    length = local_rows * ctx
    share = width // tp
    owned = w_qkv.shape[0]
    heads = w_qkv.shape[2] // HD
    slots = -(-heads // ctx)
    head_width = slots * HD
    units = w_up.shape[1] // ctx
    pad_heads = slots * ctx * HD - heads * HD

    qkv_blocks = jnp.pad(w_qkv, ((0, 0), (0, 0), (0, pad_heads)))
    qkv_blocks = qkv_blocks.reshape(owned, 3, ctx, head_width).transpose(2, 0, 1, 3)
    out_blocks = jnp.pad(w_out, ((0, 0), (0, pad_heads))).reshape(owned, ctx, head_width)
    blocks = jnp.concatenate(
        [
            w_down.reshape(owned, ctx, units).transpose(1, 0, 2),
            out_blocks.transpose(1, 0, 2),
            w_up.reshape(owned, ctx, units).transpose(1, 0, 2),
            qkv_blocks.reshape(ctx, owned, 3 * head_width),
        ],
        axis=-1,
    )
    block_width = blocks.shape[-1]
    pad_rows, pad_width = -owned % 16, -block_width % 128
    blocks = jnp.pad(blocks, ((0, 0), (0, pad_rows), (0, pad_width)))
    seg_columns = jnp.broadcast_to(segments[0].astype(bf16)[:, None], (local_rows, 128))
    packed = jnp.concatenate([inputs[0], cotangent[0], seg_columns], axis=-1)
    row, columns = gather_all(packed, blocks, dp, ctx, tp)
    columns = columns[:, :, :owned, :block_width].reshape(width, -1)
    qkv_bias = jnp.pad(b_qkv, ((0, 0), (0, pad_heads))).reshape(3, ctx, head_width)
    qkv_bias = lax.dynamic_index_in_dim(qkv_bias, my_ctx, 1, keepdims=False).reshape(-1)
    up_bias = lax.dynamic_slice_in_dim(b_up, my_ctx * units, units, 0)

    cosines, sines = angle_tables(length)
    norms = jnp.stack([gain_one, bias_one, gain_two, bias_two])
    sums, early, late, total = compute_all(
        row,
        columns,
        jnp.asarray(cosines),
        jnp.asarray(sines),
        norms,
        up_bias[None],
        qkv_bias[None],
        width,
        units,
        share,
        ctx,
        dp,
        tp,
        owned,
    )
    branch_share, input_share = sums[:, :share], sums[:, share:]
    early, late = early[:, :owned].astype(f32), late[:, :owned].astype(f32)
    own_down = early[:, :, :units].transpose(1, 0, 2).reshape(owned, -1)
    own_up = early[:, :, units : 2 * units].transpose(1, 0, 2).reshape(owned, -1)
    own_out = late[:, :, :HD].transpose(1, 0, 2).reshape(owned, -1)[:, : heads * HD]
    own_qkv = late[:, :, HD:].reshape(ctx, owned, 3, HD).transpose(1, 2, 0, 3)
    own_qkv = own_qkv.reshape(owned, 3, ctx * HD)[:, :, : heads * HD]
    total = total.reshape(-1)
    slot = 3 * HD + units
    slot += -slot % 128
    spread = total[5 * width : 5 * width + tp * ctx * slot].reshape(tp, ctx, slot)

    spread = lax.dynamic_index_in_dim(spread, my_tp, 0, keepdims=False)
    sum_b_qkv = spread[:, : 3 * head_width].reshape(ctx, 3, head_width).transpose(1, 0, 2)
    sum_b_qkv = sum_b_qkv.reshape(3, -1)[:, : heads * HD]
    sum_b_up = spread[:, 3 * head_width : 3 * head_width + units].reshape(-1)

    start = my_tp * share
    token_share = lax.dynamic_slice_in_dim(inputs[0], start, share, 1).astype(f32)
    bias_share = lax.dynamic_slice_in_dim(out_bias, start, share, 0)
    cotangent_share = lax.dynamic_slice_in_dim(cotangent[0], start, share, 1).astype(f32)
    output = token_share + branch_share + bias_share
    grad_inputs = cotangent_share + input_share
    return (
        output[None],
        grad_inputs[None],
        total[:width],
        total[width : 2 * width],
        total[2 * width : 3 * width],
        total[3 * width : 4 * width],
        own_qkv,
        sum_b_qkv,
        own_out,
        total[4 * width : 5 * width],
        own_up,
        sum_b_up,
        own_down,
    )


def solution(mesh):
    return jax.shard_map(
        on_device,
        mesh=mesh,
        in_specs=(
            P("dp", "ctx", None),
            P("dp", "ctx"),
            P(),
            P(),
            P(),
            P(),
            P(("dp", "ctx"), None, "tp"),
            P(None, "tp"),
            P(("dp", "ctx"), "tp"),
            P(),
            P(("dp", "ctx"), "tp"),
            P("tp"),
            P(("dp", "ctx"), "tp"),
            P("dp", "ctx", None),
        ),
        out_specs=(
            P("dp", "ctx", "tp"),
            P("dp", "ctx", "tp"),
            P(),
            P(),
            P(),
            P(),
            P(("dp", "ctx"), None, "tp"),
            P(None, "tp"),
            P(("dp", "ctx"), "tp"),
            P(),
            P(("dp", "ctx"), "tp"),
            P("tp"),
            P(("dp", "ctx"), "tp"),
        ),
        check_vma=False,
    )
```

```python
import functools
import math

import jax
import jax.numpy as jnp
from jax import lax
from jax.experimental import pallas as pl
from jax.experimental.pallas import tpu as pltpu
import numpy as np
from jax.sharding import PartitionSpec as P

HD = 64
ROT = 16

NORM_EPSILON = 1e-05
NEG_LARGE = -1e30
LAST = (((1,), (1,)), ((), ()))
ROWS = (((0,), (0,)), ((), ()))


def dot_f32(a, b, dims=(((1,), (0,)), ((), ()))):
    return lax.dot_general(a, b, dims, preferred_element_type=jnp.float32)


def angle_tables(length):
    frequency = np.float32(10000.0) ** (-(np.arange(ROT // 2, dtype=np.float32) * 2.0 / ROT))
    angles = np.arange(length, dtype=np.float32)[:, None] * frequency.astype(np.float32)
    rest = np.zeros((length, HD - ROT))
    angles = angles.astype(np.float64)
    cosines = np.concatenate([np.cos(angles), np.cos(angles), rest + 1.0], axis=-1)
    sines = np.concatenate([np.sin(angles), np.sin(angles), rest], axis=-1)
    return tuple(np.concatenate([t, t], axis=-1).astype(np.float32) for t in (cosines, sines))


def swap_matrix(size):
    source = lax.broadcasted_iota(jnp.int32, (size, size), 0)
    target = lax.broadcasted_iota(jnp.int32, (size, size), 1)
    dim = lax.rem(target, HD)
    half_rot = ROT // 2
    minus = (dim < half_rot) & (source == target + half_rot)
    plus = (dim >= half_rot) & (dim < ROT) & (source == target - half_rot)
    return jnp.where(plus, 1.0, 0.0) - jnp.where(minus, 1.0, 0.0)


def swapped(values, matrix):
    return lax.dot_general(
        values,
        matrix,
        (((1,), (0,)), ((), ())),
        preferred_element_type=jnp.float32,
        precision=lax.Precision.HIGHEST,
    )


class Tree:
    def __init__(self, copies, place, partial, from_core, to_x, from_x, to_z, from_z):
        self.copies, self.place, self.partial, self.from_core = copies, place, partial, from_core
        self.to_x, self.from_x, self.to_z, self.from_z = to_x, from_x, to_z, from_z
        self.over_core, self.over_x, self.over_z = {}, {}, {}

    def send_core(self, step):
        here = self.place.group(step)
        self.over_core[step] = self.copies.start(
            self.partial.at[1 - self.place.tp, here], self.from_core.at[here], self.place.sibling
        )

    def local_sum(self, step, x):
        here = self.place.token_rows(step, x)
        mine = self.partial[self.place.tp, here, :].astype(jnp.float32)
        return mine + self.from_core[here, :].astype(jnp.float32)

    def send_x(self, step):
        self.over_core[step].wait_recv()
        self.to_x[step] = self.local_sum(step, INNER - 1 - self.place.x).astype(jnp.bfloat16)
        self.over_x[step] = self.copies.start(
            self.to_x.at[step], self.from_x.at[step], self.place.partner
        )

    def x_sum(self, step):
        self.over_x[step].wait_recv()
        local = self.local_sum(step, self.place.x)
        return local + self.from_x[step].astype(jnp.float32)

    def send_z(self, step):
        self.to_z[step - 1] = self.x_sum(step).astype(jnp.bfloat16)
        self.over_z[step] = self.copies.start(
            self.to_z.at[step - 1], self.from_z.at[step - 1], self.place.along(step)
        )

    def result(self):
        total = self.x_sum(0)
        for step in range(1, self.place.outer):
            self.over_z[step].wait_recv()
            total = total + self.from_z[step - 1].astype(jnp.float32)
        return total


class Place:
    def __init__(self, ctx, dp, tp, rows):
        self.outer, self.rows = ctx // INNER, rows
        self.ctx, self.dp, self.tp = (lax.axis_index(name) for name in ("ctx", "dp", "tp"))
        self.z, self.x = self.ctx // INNER, lax.rem(self.ctx, INNER)
        self.partner = {"ctx": self.z * INNER + (INNER - 1 - self.x)}
        self.sibling = {"tp": tp - 1 - self.tp}

    def along(self, step):
        return {"ctx": lax.rem(self.z + step, self.outer) * INNER + self.x}

    def group(self, step):
        first = lax.rem(self.z + step, self.outer) * INNER * self.rows
        return pl.ds(pl.multiple_of(first, INNER * self.rows), INNER * self.rows)

    def token_rows(self, step, x):
        first = (lax.rem(self.z + step, self.outer) * INNER + x) * self.rows
        return pl.ds(pl.multiple_of(first, self.rows), self.rows)


class Exchange:
    def __init__(self, copies, place, ctx, dp, grads, from_y, summed, own_grads, local_sem):
        self.copies, self.place, self.ctx, self.dp = copies, place, ctx, dp
        self.grads, self.from_y, self.summed = grads, from_y, summed
        self.own_grads, self.local_sem = own_grads, local_sem

    def send_y(self):
        self.over_y = []
        for other in range(1, self.dp):
            target = lax.rem(self.place.dp + other, self.dp)
            self.over_y.append(
                self.copies.start(
                    self.grads.at[target], self.from_y.at[other - 1], {"dp": target}
                )
            )

    def send_ctx(self):
        for copy in self.over_y:
            copy.wait_recv()
        self.over_ctx = []
        for step in list(range(1, self.ctx)) + [0]:
            target = lax.rem(self.place.ctx + step, self.ctx)
            total = self.grads[self.place.dp, target].astype(jnp.float32)
            for other in range(1, self.dp):
                total = total + self.from_y[other - 1, target].astype(jnp.float32)
            self.summed[step] = total.astype(jnp.bfloat16)
            if step > 0:
                self.over_ctx.append(
                    self.copies.start(
                        self.summed.at[step], self.own_grads.at[self.place.ctx], {"ctx": target}
                    )
                )
        self.own = pltpu.make_async_copy(
            self.summed.at[0], self.own_grads.at[self.place.ctx], self.local_sem
        )
        self.own.start()

    def finish(self):
        for copy in self.over_ctx:
            copy.wait_recv()
        self.own.wait()


def compute_kernel(
    width,
    units,
    share,
    ctx,
    dp,
    tp,
    owned,
    row,
    columns,
    cosines,
    sines,
    norms,
    up_bias,
    qkv_bias,
    sums,
    early_own,
    late_own,
    totals,
    norm_grads,
    local_vector,
    averages,
    inverses,
    norm_one,
    norm_two,
    queries,
    keys,
    values,
    mixed,
    grad_attended,
    grad_pre,
    grad_query,
    grad_key,
    grad_value,
    grad_projected,
    hot,
    out_partial,
    out_core,
    out_to_x,
    out_from_x,
    out_to_z,
    out_from_z,
    in_partial,
    in_core,
    in_to_x,
    in_from_x,
    in_to_z,
    in_from_z,
    early_grads,
    early_y,
    early_sum,
    late_grads,
    late_y,
    late_sum,
    vectors,
    core_vector,
    x_vector,
    passed_vector,
    z_vectors,
    y_vectors,
    send_sems,
    recv_sems,
    local_sems,
):
    f32, bf16 = jnp.float32, jnp.bfloat16
    length = row.shape[0]
    rows = length // ctx
    place = Place(ctx, dp, tp, rows)
    greet(ctx, dp, tp, place.ctx, place.dp, place.tp)
    copies = Copies(send_sems, recv_sems)
    out_tree = Tree(
        copies, place, out_partial, out_core, out_to_x, out_from_x, out_to_z, out_from_z
    )
    in_tree = Tree(copies, place, in_partial, in_core, in_to_x, in_from_x, in_to_z, in_from_z)
    early = Exchange(
        copies, place, ctx, dp, early_grads, early_y, early_sum, early_own, local_sems.at[0]
    )
    late = Exchange(
        copies, place, ctx, dp, late_grads, late_y, late_sum, late_own, local_sems.at[1]
    )
    order = list(range(1, place.outer)) + [0]
    tile = INNER * rows
    tiles = length // tile
    both = units + HD
    scale = 1.0 / math.sqrt(HD)
    matrix = swap_matrix(2 * HD)
    norm_grads[...] = jnp.zeros_like(norm_grads)
    local_vector[...] = jnp.zeros_like(local_vector)
    grad_key[...] = jnp.zeros_like(grad_key)
    grad_value[...] = jnp.zeros_like(grad_value)

    def first_pass(step, carry):
        here = pl.ds(pl.multiple_of(step * tile, tile), tile)
        tokens = row[here, :width].astype(f32)
        average = jnp.mean(tokens, axis=-1, keepdims=True)
        centered = tokens - average
        variance = jnp.mean(centered * centered, axis=-1, keepdims=True)
        inverse = lax.rsqrt(variance + NORM_EPSILON)
        xhat = centered * inverse
        averages[here, :] = average
        inverses[here, :] = inverse
        one = (xhat * norms[0:1, :] + norms[1:2, :]).astype(bf16)
        two = (xhat * norms[2:3, :] + norms[3:4, :]).astype(bf16)
        norm_one[here, :] = one
        norm_two[here, :] = two
        projected = dot_f32(one, columns[:, both + units :]) + qkv_bias[...]
        turning = projected[:, : 2 * HD]
        turned = turning * cosines[here, :] + swapped(turning, matrix) * sines[here, :]
        queries[here, :] = (turned[:, :HD].astype(bf16).astype(f32) * scale).astype(bf16)
        keys[here, :] = turned[:, HD:].astype(bf16)
        values[here, :] = projected[:, 2 * HD :].astype(bf16)
        lane = lax.broadcasted_iota(jnp.int32, (tile, 128), 1).astype(f32)
        segment = row[here, 2 * width :].astype(f32)
        hot[here, :] = jnp.where(segment == lane, 1.0, 0.0).astype(bf16)
        pre = dot_f32(two, columns[:, both : both + units]) + up_bias[...]
        cumulative = 0.5 * (1.0 + lax.erf(pre * math.sqrt(0.5)))
        density = jnp.exp(pre * pre * -0.5) * (1.0 / math.sqrt(2.0 * math.pi))
        mixed[here, :units] = (pre * cumulative).astype(bf16)
        grad_mixed = dot_f32(row[here, width : 2 * width], columns[:, :both])
        slope = (grad_mixed[:, :units] * (cumulative + pre * density)).astype(bf16)
        grad_pre[here, :] = slope
        local_vector[:, 3 * HD : 3 * HD + units] += jnp.sum(slope.astype(f32), axis=0, keepdims=True)
        grad_attended[here, :] = grad_mixed[:, units:].astype(bf16)
        return carry

    lax.fori_loop(0, tiles, first_pass, 0)

    def weight_grads(store, first, left, left_first, right):
        block = ctx * owned
        for half in range(dp):
            rows_here = left[:, left_first + half * block : left_first + (half + 1) * block]
            grad = dot_f32(rows_here, right, ROWS)
            for owner in range(ctx):
                store[half, owner, :owned, first : first + right.shape[1]] = grad[
                    owner * owned : (owner + 1) * owned
                ].astype(bf16)

    weight_grads(early_grads, 0, row, width, mixed[:, :units])
    weight_grads(early_grads, units, norm_two, 0, grad_pre[...])
    early.send_y()

    for step in range(tiles):
        here = pl.ds(step * tile, tile)
        seen = (step + 1) * tile
        query, key, value = queries[here, :], keys[:seen, :], values[:seen, :]
        scores = dot_f32(query, key, LAST)
        same = dot_f32(hot[here, :], hot[:seen, :], LAST) > 0.5
        at_query = lax.broadcasted_iota(jnp.int32, (tile, seen), 0) + step * tile
        at_key = lax.broadcasted_iota(jnp.int32, (tile, seen), 1)
        scores = jnp.where(same & (at_key <= at_query), scores, NEG_LARGE)
        exponent = jnp.exp(scores - jnp.max(scores, axis=-1, keepdims=True))
        softmax = exponent / jnp.sum(exponent, axis=-1, keepdims=True)
        softmax_low = softmax.astype(bf16)
        attended = dot_f32(softmax_low, value)
        mixed[here, units:] = attended.astype(bf16)
        grad_rows = grad_attended[here, :]
        grad_dots = jnp.sum(grad_rows.astype(f32) * attended, axis=-1, keepdims=True)
        grad_probs = dot_f32(grad_rows, value, LAST)
        grad_scores = (softmax * (grad_probs - grad_dots)).astype(bf16)
        grad_query[here, :] = dot_f32(grad_scores, key) * scale
        grad_key[:, :seen] += dot_f32(query, grad_scores, ROWS)
        grad_value[:, :seen] += dot_f32(grad_rows, softmax_low, ROWS)
        if step == min(1, tiles - 1):
            early.send_ctx()

    for step in order:
        here = place.group(step)
        branch = dot_f32(mixed[here, :], columns[:, :both], LAST).astype(bf16)
        for part in range(tp):
            out_partial[part, here, :] = branch[:, part * share : (part + 1) * share]
        out_tree.send_core(step)

    for step in range(tiles):
        here = pl.ds(step * tile, tile)
        key_rows = grad_key[:, step * tile : (step + 1) * tile].T
        value_rows = grad_value[:, step * tile : (step + 1) * tile].T
        turning = jnp.concatenate([grad_query[here, :], key_rows], axis=-1)
        turned = turning * cosines[here, :] - swapped(turning, matrix) * sines[here, :]
        pulled = jnp.concatenate([turned, value_rows], axis=-1).astype(bf16)
        grad_projected[here, :] = pulled
        local_vector[:, : 3 * HD] += jnp.sum(pulled.astype(f32), axis=0, keepdims=True)

    weight_grads(late_grads, 0, row, width, mixed[:, units:])
    weight_grads(late_grads, HD, norm_one, 0, grad_projected[...])
    late.send_y()

    for step in order:
        out_tree.send_x(step)
        here = place.group(step)
        xhat = (row[here, :width].astype(f32) - averages[here, :]) * inverses[here, :]
        grad_one = dot_f32(grad_projected[here, :], columns[:, both + units :], LAST)
        grad_two = dot_f32(grad_pre[here, :], columns[:, both : both + units], LAST)
        norm_grads[0:1, :] += jnp.sum(grad_one * xhat, axis=0, keepdims=True)
        norm_grads[1:2, :] += jnp.sum(grad_one, axis=0, keepdims=True)
        norm_grads[2:3, :] += jnp.sum(grad_two * xhat, axis=0, keepdims=True)
        norm_grads[3:4, :] += jnp.sum(grad_two, axis=0, keepdims=True)
        pulled = grad_one * norms[0:1, :] + grad_two * norms[2:3, :]
        term = inverses[here, :] * (
            pulled
            - jnp.mean(pulled, axis=-1, keepdims=True)
            - xhat * jnp.mean(pulled * xhat, axis=-1, keepdims=True)
        )
        term = term.astype(bf16)
        for part in range(tp):
            in_partial[part, here, :] = term[:, part * share : (part + 1) * share]
        in_tree.send_core(step)

    for step in order:
        in_tree.send_x(step)
        if step > 0:
            out_tree.send_z(step)

    own_rows = row[place.token_rows(0, place.x), width : 2 * width].astype(f32)
    out_bias_grad = jnp.sum(own_rows, axis=0, keepdims=True)
    out_bias_grad = jnp.where(place.tp == 0, out_bias_grad, 0.0)
    vectors[...] = jnp.zeros_like(vectors)
    lines = width // 128
    for line in range(lines):
        lanes = slice(line * 128, (line + 1) * 128)
        for item in range(4):
            vectors[item * lines + line : item * lines + line + 1, :] = norm_grads[
                item : item + 1, lanes
            ]
        vectors[4 * lines + line : 4 * lines + line + 1, :] = out_bias_grad[:, lanes]
    slot_lines = local_vector.shape[1] // 128
    first_line = 5 * lines + (place.tp * ctx + place.ctx) * slot_lines
    for line in range(slot_lines):
        vectors[pl.ds(first_line + line, 1), :] = local_vector[:, line * 128 : (line + 1) * 128]
    vector_core = copies.start(vectors, core_vector, place.sibling)

    late.send_ctx()
    vector_core.wait_recv()
    passed_vector[0] = vectors[...] + core_vector[...]
    vector_x = copies.start(passed_vector.at[0], x_vector, place.partner)
    for step in range(1, place.outer):
        in_tree.send_z(step)
    vector_x.wait_recv()
    passed_vector[1] = passed_vector[0] + x_vector[...]
    z_vectors[place.z] = passed_vector[1]
    vector_z = [
        copies.start(passed_vector.at[1], z_vectors.at[place.z], place.along(step))
        for step in range(1, place.outer)
    ]
    sums[:, :share] = out_tree.result()
    for copy in vector_z:
        copy.wait_recv()
    total = z_vectors[0]
    for other in range(1, place.outer):
        total = total + z_vectors[other]
    passed_vector[2] = total
    y_vectors[place.dp] = total
    vector_y = [
        copies.start(
            passed_vector.at[2], y_vectors.at[place.dp], {"dp": lax.rem(place.dp + other, dp)}
        )
        for other in range(1, dp)
    ]
    sums[:, share:] = in_tree.result()
    for copy in vector_y:
        copy.wait_recv()
    total = y_vectors[0]
    for other in range(1, dp):
        total = total + y_vectors[other]
    totals[...] = total
    early.finish()
    late.finish()
    copies.finish()


def compute_all(
    row, columns, cosines, sines, norms, up_bias, qkv_bias, width, units, share, ctx, dp, tp, owned
):
    f32, bf16 = jnp.float32, jnp.bfloat16
    length = row.shape[0]
    outer, rows = ctx // INNER, length // ctx
    padded = owned + -owned % 16
    early_width = 2 * units + -2 * units % 128
    late_width = 4 * HD
    slot = 3 * HD + units
    slot += -slot % 128
    lines = 5 * width // 128 + tp * ctx * slot // 128
    lines += -lines % 8
    vmem = pl.BlockSpec(memory_space=pltpu.VMEM)
    anywhere = pl.BlockSpec(memory_space=pl.ANY)
    tree = [
        pltpu.VMEM((tp, length, share), bf16),
        pltpu.VMEM((length, share), bf16),
        pltpu.VMEM((outer, rows, share), bf16),
        pltpu.VMEM((outer, rows, share), bf16),
        pltpu.VMEM((outer - 1, rows, share), bf16),
        pltpu.VMEM((outer - 1, rows, share), bf16),
    ]

    def exchange(block_width):
        return [
            pltpu.VMEM((dp, ctx, padded, block_width), bf16),
            pltpu.VMEM((dp - 1, ctx, padded, block_width), bf16),
            pltpu.VMEM((ctx, padded, block_width), bf16),
        ]

    count = 2 * (3 * outer - 1) + 2 * (dp - 1 + ctx - 1) + 2 + (outer - 1) + (dp - 1)
    vector = (lines, 128)
    return pl.pallas_call(
        functools.partial(compute_kernel, width, units, share, ctx, dp, tp, owned),
        out_shape=(
            jax.ShapeDtypeStruct((rows, 2 * share), f32),
            jax.ShapeDtypeStruct((ctx, padded, early_width), bf16),
            jax.ShapeDtypeStruct((ctx, padded, late_width), bf16),
            jax.ShapeDtypeStruct(vector, f32),
        ),
        in_specs=[vmem] * 7,
        out_specs=(vmem, anywhere, anywhere, vmem),
        scratch_shapes=[
            pltpu.VMEM((4, width), f32),
            pltpu.VMEM((1, slot), f32),
            pltpu.VMEM((length, 1), f32),
            pltpu.VMEM((length, 1), f32),
            pltpu.VMEM((length, width), bf16),
            pltpu.VMEM((length, width), bf16),
            pltpu.VMEM((length, HD), bf16),
            pltpu.VMEM((length, HD), bf16),
            pltpu.VMEM((length, HD), bf16),
            pltpu.VMEM((length, units + HD), bf16),
            pltpu.VMEM((length, HD), bf16),
            pltpu.VMEM((length, units), bf16),
            pltpu.VMEM((length, HD), f32),
            pltpu.VMEM((HD, length), f32),
            pltpu.VMEM((HD, length), f32),
            pltpu.VMEM((length, 3 * HD), bf16),
            pltpu.VMEM((length, 128), bf16),
        ]
        + tree
        + tree
        + exchange(early_width)
        + exchange(late_width)
        + [
            pltpu.VMEM(vector, f32),
            pltpu.VMEM(vector, f32),
            pltpu.VMEM(vector, f32),
            pltpu.VMEM((3,) + vector, f32),
            pltpu.VMEM((outer,) + vector, f32),
            pltpu.VMEM((dp,) + vector, f32),
            pltpu.SemaphoreType.DMA((count,)),
            pltpu.SemaphoreType.DMA((count,)),
            pltpu.SemaphoreType.DMA((2,)),
        ],
        compiler_params=pltpu.CompilerParams(
            collective_id=1, has_side_effects=True, vmem_limit_bytes=60 * 2**20
        ),
    )(row, columns, cosines, sines, norms, up_bias, qkv_bias)


MESH = pl.DeviceIdType.MESH
INNER = 2


def greet(ctx, dp, tp, my_ctx, my_dp, my_tp):
    barrier = pltpu.get_barrier_semaphore()
    for step in range(1, ctx):
        peer = {"ctx": lax.rem(my_ctx + step, ctx)}
        pl.semaphore_signal(barrier, inc=1, device_id=peer, device_id_type=MESH)
    for step in range(1, dp):
        peer = {"dp": lax.rem(my_dp + step, dp)}
        pl.semaphore_signal(barrier, inc=1, device_id=peer, device_id_type=MESH)
    for step in range(1, tp):
        peer = {"tp": lax.rem(my_tp + step, tp)}
        pl.semaphore_signal(barrier, inc=1, device_id=peer, device_id_type=MESH)
    pl.semaphore_wait(barrier, ctx + dp + tp - 3)


class Copies:
    def __init__(self, send_sems, recv_sems):
        self.send_sems, self.recv_sems, self.items = send_sems, recv_sems, []

    def start(self, src, dst, peer):
        place = len(self.items)
        copy = pltpu.make_async_remote_copy(
            src_ref=src,
            dst_ref=dst,
            send_sem=self.send_sems.at[place],
            recv_sem=self.recv_sems.at[place],
            device_id=peer,
            device_id_type=MESH,
        )
        copy.start()
        self.items.append(copy)
        return copy

    def finish(self):
        for copy in self.items:
            copy.wait_send()


def gather_kernel(
    ctx,
    dp,
    tp,
    packed,
    blocks,
    row,
    columns,
    send_sems,
    recv_sems,
    line_send,
    line_recv,
    x_send,
    x_recv,
    core_send,
    core_recv,
    local_sems,
):
    my_ctx, my_dp, my_tp = lax.axis_index("ctx"), lax.axis_index("dp"), lax.axis_index("tp")
    outer = ctx // INNER
    my_z, my_x = my_ctx // INNER, lax.rem(my_ctx, INNER)
    other_x = INNER - 1 - my_x
    rows = packed.shape[0]
    half = rows // tp

    def piece(owner, core):
        return row.at[pl.ds(pl.multiple_of(owner * rows + core * half, half), half)]

    own_row = pltpu.make_async_copy(
        packed, row.at[pl.ds(pl.multiple_of(my_ctx * rows, rows), rows)], local_sems.at[0]
    )
    own_block = pltpu.make_async_copy(
        blocks.at[my_ctx], columns.at[my_dp, my_ctx], local_sems.at[1]
    )
    own_row.start()
    own_block.start()
    greet(ctx, dp, tp, my_ctx, my_dp, my_tp)
    copies = Copies(send_sems, recv_sems)
    mine = packed.at[pl.ds(pl.multiple_of(my_tp * half, half), half)]
    partner = {"ctx": my_z * INNER + other_x}
    sibling = {"tp": tp - 1 - my_tp}

    def inside(place):
        return (place >= 0) & (place < outer)

    def hop(way, step):
        place = 0 if way > 0 else 1
        shard = (my_z - way * step) * INNER + my_x
        return pltpu.make_async_remote_copy(
            src_ref=mine if step == 0 else piece(shard, my_tp),
            dst_ref=piece(shard, my_tp),
            send_sem=line_send.at[place, step],
            recv_sem=line_recv.at[place, step],
            device_id={"ctx": (my_z + way) * INNER + my_x},
            device_id_type=MESH,
        )

    def hops_on(way, step):
        return inside(my_z - way * step) & inside(my_z + way)

    def cross(shard_z, own):
        shard = shard_z * INNER + my_x
        return pltpu.make_async_remote_copy(
            src_ref=mine if own else piece(shard, my_tp),
            dst_ref=piece(shard, my_tp),
            send_sem=x_send.at[shard_z],
            recv_sem=x_recv.at[shard_z],
            device_id=partner,
            device_id_type=MESH,
        )

    def to_sibling(shard):
        return pltpu.make_async_remote_copy(
            src_ref=piece(shard, my_tp),
            dst_ref=piece(shard, my_tp),
            send_sem=core_send.at[shard],
            recv_sem=core_recv.at[shard],
            device_id=sibling,
            device_id_type=MESH,
        )

    for way in (1, -1):

        @pl.when(hops_on(way, 0))
        def _(way=way):
            hop(way, 0).start()

    cross(my_z, True).start()
    for step in range(1, outer):
        for way in (1, -1):

            @pl.when(inside(my_z - way * step))
            def _(way=way, step=step):
                hop(way, step - 1).wait_recv()
                if step < outer - 1:

                    @pl.when(inside(my_z + way))
                    def _():
                        hop(way, step).start()

                shard_z = my_z - way * step
                cross(shard_z, False).start()
                to_sibling(shard_z * INNER + my_x).start()

    exchanged = []
    for step in range(1, ctx):
        target = lax.rem(my_ctx + step, ctx)
        exchanged.append(
            copies.start(blocks.at[target], columns.at[my_dp, my_ctx], {"ctx": target})
        )
    over_dp = []
    for other in range(1, dp):
        target = {"dp": lax.rem(my_dp + other, dp)}
        over_dp.append(
            copies.start(blocks.at[my_ctx], columns.at[my_dp, my_ctx], target)
        )
    for step in range(outer):
        for way in (1, -1) if step > 0 else (1,):

            @pl.when(inside(my_z - way * step))
            def _(way=way, step=step):
                shard_z = my_z - way * step
                cross(shard_z, False).wait_recv()
                to_sibling(shard_z * INNER + other_x).start()

    for step in range(1, ctx):
        source = lax.rem(my_ctx + ctx - step, ctx)
        exchanged[step - 1].wait_recv()
        for other in range(1, dp):
            target = {"dp": lax.rem(my_dp + other, dp)}
            over_dp.append(
                copies.start(columns.at[my_dp, source], columns.at[my_dp, source], target)
            )
    for step in range(1, ctx):
        copy = to_sibling(lax.rem(my_ctx + step, ctx))
        copy.wait_recv()
        copy.wait_send()
    for copy in over_dp:
        copy.wait_recv()
    copies.finish()
    for shard_z in range(outer):
        cross(shard_z, False).wait_send()
    for step in range(outer - 1):
        for way in (1, -1):

            @pl.when(hops_on(way, step))
            def _(way=way, step=step):
                hop(way, step).wait_send()

    own_row.wait()
    own_block.wait()


def gather_all(packed, blocks, dp, ctx, tp):
    outer = ctx // INNER
    count = (ctx - 1) + ctx * (dp - 1)
    return pl.pallas_call(
        functools.partial(gather_kernel, ctx, dp, tp),
        out_shape=(
            jax.ShapeDtypeStruct((ctx * packed.shape[0], packed.shape[1]), packed.dtype),
            jax.ShapeDtypeStruct((dp,) + blocks.shape, blocks.dtype),
        ),
        in_specs=[pl.BlockSpec(memory_space=pl.ANY)] * 2,
        out_specs=(pl.BlockSpec(memory_space=pl.ANY),) * 2,
        scratch_shapes=[
            pltpu.SemaphoreType.DMA((count,)),
            pltpu.SemaphoreType.DMA((count,)),
            pltpu.SemaphoreType.DMA((2, outer - 1)),
            pltpu.SemaphoreType.DMA((2, outer - 1)),
            pltpu.SemaphoreType.DMA((outer,)),
            pltpu.SemaphoreType.DMA((outer,)),
            pltpu.SemaphoreType.DMA((ctx,)),
            pltpu.SemaphoreType.DMA((ctx,)),
            pltpu.SemaphoreType.DMA((2,)),
        ],
        compiler_params=pltpu.CompilerParams(collective_id=0, has_side_effects=True),
    )(packed, blocks)


def on_device(
    inputs,
    segments,
    gain_one,
    bias_one,
    gain_two,
    bias_two,
    w_qkv,
    b_qkv,
    w_out,
    out_bias,
    w_up,
    b_up,
    w_down,
    cotangent,
):
    f32, bf16 = jnp.float32, jnp.bfloat16
    dp, ctx, tp = lax.axis_size("dp"), lax.axis_size("ctx"), lax.axis_size("tp")
    my_ctx, my_tp = lax.axis_index("ctx"), lax.axis_index("tp")
    local_rows, width = inputs.shape[1:]
    length = local_rows * ctx
    share = width // tp
    owned = w_qkv.shape[0]
    heads = w_qkv.shape[2] // HD
    slots = -(-heads // ctx)
    head_width = slots * HD
    units = w_up.shape[1] // ctx
    pad_heads = slots * ctx * HD - heads * HD

    qkv_blocks = jnp.pad(w_qkv, ((0, 0), (0, 0), (0, pad_heads)))
    qkv_blocks = qkv_blocks.reshape(owned, 3, ctx, head_width).transpose(2, 0, 1, 3)
    out_blocks = jnp.pad(w_out, ((0, 0), (0, pad_heads))).reshape(owned, ctx, head_width)
    blocks = jnp.concatenate(
        [
            w_down.reshape(owned, ctx, units).transpose(1, 0, 2),
            out_blocks.transpose(1, 0, 2),
            w_up.reshape(owned, ctx, units).transpose(1, 0, 2),
            qkv_blocks.reshape(ctx, owned, 3 * head_width),
        ],
        axis=-1,
    )
    block_width = blocks.shape[-1]
    pad_rows, pad_width = -owned % 16, -block_width % 128
    blocks = jnp.pad(blocks, ((0, 0), (0, pad_rows), (0, pad_width)))
    seg_columns = jnp.broadcast_to(segments[0].astype(bf16)[:, None], (local_rows, 128))
    packed = jnp.concatenate([inputs[0], cotangent[0], seg_columns], axis=-1)
    row, columns = gather_all(packed, blocks, dp, ctx, tp)
    columns = columns[:, :, :owned, :block_width].reshape(width, -1)
    qkv_bias = jnp.pad(b_qkv, ((0, 0), (0, pad_heads))).reshape(3, ctx, head_width)
    qkv_bias = lax.dynamic_index_in_dim(qkv_bias, my_ctx, 1, keepdims=False).reshape(-1)
    up_bias = lax.dynamic_slice_in_dim(b_up, my_ctx * units, units, 0)

    cosines, sines = angle_tables(length)
    norms = jnp.stack([gain_one, bias_one, gain_two, bias_two])
    sums, early, late, total = compute_all(
        row,
        columns,
        jnp.asarray(cosines),
        jnp.asarray(sines),
        norms,
        up_bias[None],
        qkv_bias[None],
        width,
        units,
        share,
        ctx,
        dp,
        tp,
        owned,
    )
    branch_share, input_share = sums[:, :share], sums[:, share:]
    early, late = early[:, :owned].astype(f32), late[:, :owned].astype(f32)
    own_down = early[:, :, :units].transpose(1, 0, 2).reshape(owned, -1)
    own_up = early[:, :, units : 2 * units].transpose(1, 0, 2).reshape(owned, -1)
    own_out = late[:, :, :HD].transpose(1, 0, 2).reshape(owned, -1)[:, : heads * HD]
    own_qkv = late[:, :, HD:].reshape(ctx, owned, 3, HD).transpose(1, 2, 0, 3)
    own_qkv = own_qkv.reshape(owned, 3, ctx * HD)[:, :, : heads * HD]
    total = total.reshape(-1)
    slot = 3 * HD + units
    slot += -slot % 128
    spread = total[5 * width : 5 * width + tp * ctx * slot].reshape(tp, ctx, slot)

    spread = lax.dynamic_index_in_dim(spread, my_tp, 0, keepdims=False)
    sum_b_qkv = spread[:, : 3 * head_width].reshape(ctx, 3, head_width).transpose(1, 0, 2)
    sum_b_qkv = sum_b_qkv.reshape(3, -1)[:, : heads * HD]
    sum_b_up = spread[:, 3 * head_width : 3 * head_width + units].reshape(-1)

    start = my_tp * share
    token_share = lax.dynamic_slice_in_dim(inputs[0], start, share, 1).astype(f32)
    bias_share = lax.dynamic_slice_in_dim(out_bias, start, share, 0)
    cotangent_share = lax.dynamic_slice_in_dim(cotangent[0], start, share, 1).astype(f32)
    output = token_share + branch_share + bias_share
    grad_inputs = cotangent_share + input_share
    return (
        output[None],
        grad_inputs[None],
        total[:width],
        total[width : 2 * width],
        total[2 * width : 3 * width],
        total[3 * width : 4 * width],
        own_qkv,
        sum_b_qkv,
        own_out,
        total[4 * width : 5 * width],
        own_up,
        sum_b_up,
        own_down,
    )


def solution(mesh):
    return jax.shard_map(
        on_device,
        mesh=mesh,
        in_specs=(
            P("dp", "ctx", None),
            P("dp", "ctx"),
            P(),
            P(),
            P(),
            P(),
            P(("dp", "ctx"), None, "tp"),
            P(None, "tp"),
            P(("dp", "ctx"), "tp"),
            P(),
            P(("dp", "ctx"), "tp"),
            P("tp"),
            P(("dp", "ctx"), "tp"),
            P("dp", "ctx", None),
        ),
        out_specs=(
            P("dp", "ctx", "tp"),
            P("dp", "ctx", "tp"),
            P(),
            P(),
            P(),
            P(),
            P(("dp", "ctx"), None, "tp"),
            P(None, "tp"),
            P(("dp", "ctx"), "tp"),
            P(),
            P(("dp", "ctx"), "tp"),
            P("tp"),
            P(("dp", "ctx"), "tp"),
        ),
        check_vma=False,
    )
```
